32 devices in a mesh: groups: 2 (over x), psg: 16 (over z, y, core).
Axes of the slice: x: 2, y: 2, z: 4, core: 2. Of those that a mesh axis runs over, the one named last changes fastest.
Arguments:
- passage_states: bfloat16 [16384, 1024], P(('groups', 'psg')), parts along dimension 0, may hold values from -6 to 6
- saved_preact: bfloat16 [16384, 2048], P(('groups', 'psg')), parts along dimension 0, may hold values from -6 to 6
- saved_resid: bfloat16 [16384, 1024], P(('groups', 'psg')), parts along dimension 0, may hold values from -84 to 84
- w_in: bfloat16 [2048, 1024], P('psg'), may hold values from -0.1875 to 0.1875
- w_out: bfloat16 [2048, 1024], P('psg'), may hold values from -0.125 to 0.125
- norm_gain: float32 [1024], replicated, may hold values from 0.1 to 1.9
- query_emb: bfloat16 [64, 1024], P(('groups', 'psg')), parts along dimension 0, may hold values from -8 to 8
- score_grads: bfloat16 [64, 32], P(('groups', 'psg')), parts along dimension 0, may hold values from -6 to 6
- retrieved: int32 [64, 32], P(('groups', 'psg')), parts along dimension 0, may hold values from 0 to 63, all different within a row
- placement_map: int32 [128], P('groups'), parts along dimension 0, may hold values from 0 to 63, each once
- live_counts: int32 [32], P('groups'), parts along dimension 0, may hold values from 1 to 4, 40 in all
Outputs:
- input_grad: bfloat16 [16384, 1024], P(('groups', 'psg')), parts along dimension 0
- grad_in: float32 [4096, 1024], P(('groups', 'psg')), parts along dimension 0
- grad_out: float32 [4096, 1024], P(('groups', 'psg')), parts along dimension 0
- question_grad: float32 [64, 1024], P(('groups', 'psg')), parts along dimension 0
The draws below stay inside these ranges and needn't reach their ends.
There are 2 independent parts, one for each index of `groups`. The reference program is written for one: setup_inputs(seed, part) draws one part's arguments, and reference() takes and returns one part's arrays. A program takes and returns all parts, laid end to end along the dimension named above; an argument that names none is the same for every part. Nothing has to cross between parts.
Inputs may be any that keep to these rules, and one draw needn't show every extreme that they name: `retrieved`: each row names 32 different passage ids. `placement_map`: storage place p means slot p mod 4 of owner p div 4, tokens p * 128 onward of the passage arrays. Owner o holds live passages in its slots 0 to live_counts[o] - 1; pairs placed in other slots contribute nothing.
All inputs are finite; a program needn't handle non-finite values.
Results may differ from the reference program's by a relative error of at most 0.007.
Values may be sent and summed in bfloat16 or wider, within the bound.
No kernel may reach another device: no remote copies, remote signals or barrier semaphores. Data moves between devices by JAX's collectives and lax.ppermute only.
A program may use at most 128 MiB of HBM per device.

```python
import math
import jax
import jax.numpy as jnp
import numpy as np
from jax import lax

D = 1024
FF = 2048
LEN = 128
K = 32
SLOTS = 4
OWNERS = 16
NPASS = 64
PASS_TOK = 8192
QUESTIONS = 32
N_PSG = 16


def shared_direction(key):
    key = jax.random.fold_in(key, 101)
    return jnp.clip(jax.random.normal(key, (1, D), jnp.float32), -2.5, 2.5)


def draw_saved_resid(key, part):
    direction = shared_direction(key)
    key = jax.random.fold_in(key, 7)
    noise_key = jax.random.fold_in(key, 0)
    scale_key = jax.random.fold_in(key, 1)
    coupling_key = jax.random.fold_in(key, 3)
    parity_key = jax.random.fold_in(key, 4)
    row_scale = jnp.exp(jax.random.uniform(scale_key, (PASS_TOK, 1), jnp.float32, 0.0, math.log(12.0)))
    parity = (2 * jax.random.randint(parity_key, (PASS_TOK, 1), 0, 2) - 1).astype(jnp.float32)
    coupling = jax.random.uniform(coupling_key, (PASS_TOK, 1), jnp.float32, 0.4, 1.0) * parity
    noise = jnp.clip(jax.random.normal(noise_key, (PASS_TOK, D), jnp.float32), -6.0, 6.0)
    values = jnp.clip(noise + coupling * direction, -7.0, 7.0)
    return (values * row_scale).astype(jnp.bfloat16)


def draw_query_emb(key, part):
    direction = shared_direction(key)
    key = jax.random.fold_in(key, 11)
    coef_key, noise_key = jax.random.split(key, 2)
    strength = jax.random.uniform(coef_key, (QUESTIONS, 1), jnp.float32, 1.0, 2.0)
    noise = jnp.clip(jax.random.normal(noise_key, (QUESTIONS, D), jnp.float32), -4.0, 4.0)
    return jnp.clip(strength * direction + noise, -8.0, 8.0).astype(jnp.bfloat16)


def spiked(entries, own_key, source, target, parts, factor):
    def block_of(dim):
        return (jnp.arange(entries.shape[dim]) // (entries.shape[dim] // parts)).reshape((-1,) + (1,) * (entries.ndim - 1 - dim))

    near = jax.random.permutation(own_key, parts)[block_of(target)]
    second = (block_of(target) + parts // 2) % parts
    return jnp.where((block_of(source) == near) | (block_of(source) == second), factor * entries, entries)


def level_of(rng, extent, cuts, smallest, largest):
    level, own = 1.0, jax.random.fold_in(rng, 6)
    for dim, blocks in cuts:
        steps = jnp.exp(jax.random.uniform(jax.random.fold_in(own, dim), (blocks,), jnp.float32, smallest / len(cuts), largest / len(cuts)))
        level = level * jnp.repeat(steps, extent[dim] // blocks).reshape([-1 if axis == dim else 1 for axis in range(len(extent))])
    return level


def distinct(own_key, rows, count, top, lift):
    order = jax.random.permutation(jax.random.fold_in(own_key, 1), count)
    boost = order
    for power in range(3):
        boost = boost * boost // count
    boost = boost * lift // count
    lots = jax.random.randint(jax.random.fold_in(own_key, 2), (rows, count), 0, 4096) + boost
    sure = jax.random.permutation(jax.random.fold_in(own_key, 3), rows)[jnp.arange(count) % rows]
    lots = jnp.where(jnp.arange(rows)[:, None] == sure[None, :], 1 << 14, lots)
    score = lots * count + jnp.arange(count)
    return lax.top_k(score.astype(jnp.int32), top)[1].astype(jnp.int32)


def profile(count, total, bound, slope):
    loads = [(1 << 20) // math.isqrt(rank ** slope) + 1 for rank in range(2, count + 1)]
    spare, counts = total - bound - (count - 1), [1] * (count - 1)
    while spare > 0:
        movable = [i for i in range(count - 1) if counts[i] < bound]
        pool, left = sum([loads[i] for i in movable]), spare
        for i in movable:
            more = min(bound - counts[i], max(1, left * loads[i] // pool), spare)
            counts[i] = counts[i] + more
            spare = spare - more
    return np.array([bound] + counts)


def ragged_sizes(stream_key, count, total, most, slope):
    if count == 2:
        one = jax.random.randint(stream_key, (), max(1, total - most), min(most, total - 1) + 1)
        return jnp.stack([one, total - one])
    lengths = jnp.asarray(profile(count, total, most, slope), jnp.int32)
    pairs = (count - 1) // 2
    donor, sink = lengths[1:1 + 2 * pairs:2], lengths[2:2 + 2 * pairs:2]
    slack = jnp.minimum(donor - 1, most - sink)
    moved = jax.random.randint(jax.random.fold_in(stream_key, 1), (pairs,), 0, 1 << 20) % (slack + 1)
    lengths = lengths.at[1:1 + 2 * pairs:2].set(donor - moved).at[2:2 + 2 * pairs:2].set(sink + moved)
    return lengths[jax.random.permutation(jax.random.fold_in(stream_key, 2), count)]


def normal_values(rng, dims, spread, bound, shards=(), dtype=jnp.bfloat16):
    factor_of = level_of(rng, dims, shards, -0.22, 0.18) if shards else 1.0
    drawn = jax.random.normal(rng, dims, jnp.float32) * spread * factor_of
    return jnp.minimum(jnp.maximum(drawn, -bound), bound).astype(dtype)


def noise_with(rng, dims, deviation, limit, cuts, heavy, kind=jnp.bfloat16):
    entries = deviation * jax.random.normal(rng, dims, jnp.float32)
    if cuts:
        entries = entries * level_of(rng, dims, cuts, -0.22, 0.18)
    return jnp.clip(spiked(entries, jax.random.fold_in(rng, 3), *heavy), -limit, limit).astype(kind)


def setup_inputs(seed: int = 0, part: int = 0) -> dict:
    arg_keys = jax.random.split(jax.random.key(seed), 12)
    part_splits = jax.random.split(jax.random.fold_in(arg_keys[11], part), 12)
    passage_states = normal_values(part_splits[0], (PASS_TOK, D), 1.0, 6.0, ((0, 16),))
    saved_preact = noise_with(part_splits[1], (PASS_TOK, FF), 1.0, 6.0, ((0, 16),), (0, 1, 16, 2.0))
    saved_resid = draw_saved_resid(jax.random.fold_in(jax.random.fold_in(arg_keys[11], part), 71), part)
    w_in = normal_values(arg_keys[3], (FF, D), D ** -0.5, 0.1875, ((0, 16),))
    w_out = normal_values(arg_keys[4], (FF, D), FF ** -0.5, 0.125, ((0, 16),))
    norm_gain = jnp.clip(1.0 + 0.18 * jax.random.normal(arg_keys[5], (D,), jnp.float32), 0.1, 1.9)
    query_emb = draw_query_emb(jax.random.fold_in(jax.random.fold_in(arg_keys[11], part), 71), part)
    score_grads = normal_values(part_splits[7], (QUESTIONS, K), 1.0, 6.0, ((0, 16),))
    retrieved = distinct(part_splits[8], QUESTIONS, NPASS, K, 4096)
    placement_map = jax.random.permutation(part_splits[9], NPASS).astype(jnp.int32)
    live_counts = ragged_sizes(part_splits[10], OWNERS, N_PSG * (SLOTS + 1) // 2, SLOTS, 2).astype(jnp.int32)
    return {"passage_states": passage_states, "saved_preact": saved_preact, "saved_resid": saved_resid, "w_in": w_in, "w_out": w_out, "norm_gain": norm_gain, "query_emb": query_emb, "score_grads": score_grads, "retrieved": retrieved, "placement_map": placement_map, "live_counts": live_counts}


def gelu_terms(preact):
    cdf = 0.5 * (1.0 + jax.scipy.special.erf(preact * 0.7071067811865476))
    density = jnp.exp(-0.5 * preact * preact) * 0.3989422804014327
    return (preact * cdf, cdf + preact * density)

def normalize(resid):
    values = resid.astype(jnp.float32)
    centre = values - lax.optimization_barrier(jnp.mean(values, axis=-1, keepdims=True))
    inverse = lax.rsqrt(lax.optimization_barrier(jnp.mean(centre * centre, axis=-1, keepdims=True)) + 1e-06)
    return (centre * inverse, inverse)

def reference(passage_states, saved_preact, saved_resid, w_in, w_out, norm_gain, query_emb, score_grads, retrieved, placement_map, live_counts):
    highest = lax.Precision.HIGHEST
    normed, inverse = normalize(saved_resid)
    pooled = (normed * norm_gain).reshape(NPASS, LEN, D).mean(axis=1).astype(jnp.bfloat16)
    placed = placement_map[retrieved].astype(jnp.int32)
    alive = placed % SLOTS < live_counts[placed // SLOTS]
    weights = jnp.where(alive, score_grads.astype(jnp.float32), 0.0)
    question_ids = lax.broadcasted_iota(jnp.int32, (QUESTIONS, K), 0)
    pair_matrix = jnp.zeros((NPASS, QUESTIONS), jnp.float32).at[placed, question_ids].add(weights)
    pair_bf = pair_matrix.astype(jnp.bfloat16).astype(jnp.float32)
    pass_grad = jnp.dot(pair_bf, query_emb.astype(jnp.float32), precision=highest)
    question_grad = jnp.dot(pair_bf.T, pooled.astype(jnp.float32), precision=highest)
    token_grad = jnp.broadcast_to((pass_grad / LEN)[:, None, :], (NPASS, LEN, D)).reshape(PASS_TOK, D)
    scaled = token_grad * norm_gain
    resid_grad = inverse * (scaled - lax.optimization_barrier(jnp.mean(scaled, axis=-1, keepdims=True)) - normed * lax.optimization_barrier(jnp.mean(scaled * normed, axis=-1, keepdims=True)))
    resid_bf = resid_grad.astype(jnp.bfloat16).astype(jnp.float32)
    activated, gelu_slope = gelu_terms(saved_preact.astype(jnp.float32))
    act_bf = activated.astype(jnp.bfloat16).astype(jnp.float32)
    hidden_grad = jnp.dot(resid_bf, w_out.astype(jnp.float32).T, precision=highest)
    pre_grad = (hidden_grad * gelu_slope).astype(jnp.bfloat16).astype(jnp.float32)
    input_grad = (jnp.dot(pre_grad, w_in.astype(jnp.float32), precision=highest) + resid_grad).astype(jnp.bfloat16)
    grad_in = jnp.dot(pre_grad.T, passage_states.astype(jnp.float32), precision=highest)
    grad_out = jnp.dot(act_bf.T, resid_bf, precision=highest)
    return (input_grad, grad_in, grad_out, question_grad)
```

```python
import functools

import jax
import jax.numpy as jnp
from jax import lax
from jax.experimental import pallas as pl
from jax.experimental.pallas import tpu as pltpu
from jax.sharding import PartitionSpec as P

LEN = 128
BF = jnp.bfloat16
F32 = jnp.float32
VMEM_LIMIT = 40 << 20


def params(**kw):
    return pltpu.CompilerParams(vmem_limit_bytes=VMEM_LIMIT, **kw)


def cost(flops, nbytes):
    return pl.CostEstimate(flops=int(flops), bytes_accessed=int(nbytes), transcendentals=0)


def swap(x, mask):
    n = lax.axis_size("psg")
    return lax.ppermute(x, "psg", [(i, i ^ mask) for i in range(n)])


def pack_kernel(slots, d_ref, place_ref, live_ref, resid_ref, gain_ref, query_ref, score_ref, ret_ref, out_ref):
    me = d_ref[0]
    passages = place_ref.shape[0]
    width = out_ref.shape[1]
    queries, picks = ret_ref.shape
    ids = ret_ref[...]

    def look(i, placed):
        p = place_ref[i]
        owner = p // slots
        slot = p % slots
        rel = (owner ^ me) * slots + slot
        rel = jnp.where(slot < live_ref[owner], rel, -1)
        return jnp.where(ids == i, rel, placed)

    placed = lax.fori_loop(0, passages, look, jnp.full(ids.shape, -1, jnp.int32), unroll=8)
    score = score_ref[...].astype(F32)
    lanes = max(passages, 128)
    cols = lax.broadcasted_iota(jnp.int32, (queries, lanes), 1)
    pairs = jnp.zeros((queries, lanes), F32)
    for k in range(picks):
        pairs = pairs + jnp.where(cols == placed[:, k : k + 1], score[:, k : k + 1], 0.0)
    if lanes < width:
        pairs = jnp.concatenate([pairs, jnp.zeros((queries, width - lanes), F32)], axis=1)
    rows = []
    for s in range(slots):
        x = resid_ref[s * LEN : (s + 1) * LEN, :].astype(F32)
        centre = x - jnp.mean(x, axis=-1, keepdims=True)
        inverse = lax.rsqrt(jnp.mean(centre * centre, axis=-1, keepdims=True) + 1e-06)
        rows.append(jnp.mean(centre * inverse, axis=0, keepdims=True) * gain_ref[...])
    out_ref[...] = jnp.concatenate(rows + [query_ref[...].astype(F32), pairs], axis=0).astype(BF)


def pack(slots, me, placement, live, resid, gain, query, score, retrieved):
    width = resid.shape[1]
    queries = query.shape[0]
    smem = pl.BlockSpec(memory_space=pltpu.SMEM)
    vmem = pl.BlockSpec(memory_space=pltpu.VMEM)
    return pl.pallas_call(
        functools.partial(pack_kernel, slots),
        out_shape=jax.ShapeDtypeStruct((slots + 2 * queries, width), BF),
        in_specs=[smem] * 3 + [vmem] * 5,
        out_specs=vmem,
        compiler_params=params(),
        cost_estimate=cost(1e6, 3e6),
        name="pack",
    )(me, placement, live, resid, gain, query, score, retrieved)


def resid_kernel(slots, queries, own_ref, nb_ref, all_ref, gain_ref, bf_ref, full_ref, question_ref, pass_ref):
    step = pl.program_id(0)
    rows = slots + 2 * queries
    total = all_ref.shape[0]
    lanes = max(total // rows * slots, 128)

    @pl.when(step == 0)
    def _():
        table = all_ref[...]
        head = all_ref[:, :lanes].astype(F32)
        r = lax.broadcasted_iota(jnp.int32, (total, lanes), 0)
        c = lax.broadcasted_iota(jnp.int32, (total, lanes), 1)
        inside = r % rows
        moved = pltpu.roll(head, total - queries, 0)
        is_query = (inside >= slots) & (inside < slots + queries)
        fc = lax.broadcasted_iota(jnp.int32, (lanes, 128), 0)
        fs = lax.broadcasted_iota(jnp.int32, (lanes, 128), 1)
        picked = jnp.zeros((total, 128), F32)
        for k in range(2):
            mine = jnp.where(is_query & (c // slots == ((r // rows) ^ k)), moved, 0.0).astype(BF)
            fold = ((fc % slots + k * slots) == fs).astype(F32).astype(BF)
            picked = picked + jnp.dot(mine, fold, preferred_element_type=F32)
        grads = lax.dot_general(
            picked.astype(BF), table, (((0,), (0,)), ((), ())), preferred_element_type=F32
        )
        pass_ref[...] = grads[: 2 * slots] * gain_ref[...] * (1.0 / LEN)
        own = head[:rows]
        ec = lax.broadcasted_iota(jnp.int32, (lanes, total), 0)
        er = lax.broadcasted_iota(jnp.int32, (lanes, total), 1)
        spread = ((er // rows == ec // slots) & (er % rows == ec % slots)).astype(F32).astype(BF)
        weights = jnp.dot(own.astype(BF), spread, preferred_element_type=F32).astype(BF)
        result = jnp.dot(weights, table, preferred_element_type=F32)
        question_ref[...] = result[slots + queries :]

    for k, src in enumerate((own_ref, nb_ref)):
        x = src[...].astype(F32)
        centre = x - jnp.mean(x, axis=-1, keepdims=True)
        inverse = lax.rsqrt(jnp.mean(centre * centre, axis=-1, keepdims=True) + 1e-06)
        normed = centre * inverse
        scaled = pass_ref[pl.ds(k * slots + step, 1), :]
        base = scaled - jnp.mean(scaled, axis=-1, keepdims=True)
        grad = inverse * (base - normed * jnp.mean(scaled * normed, axis=-1, keepdims=True))
        bf_ref[k] = grad.astype(BF)
        if k == 0:
            full_ref[...] = grad


def resid_grads(slots, queries, own, nb, table, gain):
    tokens, width = own.shape
    total = table.shape[0]
    return pl.pallas_call(
        functools.partial(resid_kernel, slots, queries),
        grid=(slots,),
        out_shape=(
            jax.ShapeDtypeStruct((2, tokens, width), BF),
            jax.ShapeDtypeStruct((tokens, width), F32),
            jax.ShapeDtypeStruct((queries, width), F32),
        ),
        in_specs=[
            pl.BlockSpec((LEN, width), lambda s: (s, 0)),
            pl.BlockSpec((LEN, width), lambda s: (s, 0)),
            pl.BlockSpec((total, width), lambda s: (0, 0)),
            pl.BlockSpec((1, width), lambda s: (0, 0)),
        ],
        out_specs=(
            pl.BlockSpec((2, LEN, width), lambda s: (0, s, 0)),
            pl.BlockSpec((LEN, width), lambda s: (s, 0)),
            pl.BlockSpec((queries, width), lambda s: (0, 0)),
        ),
        scratch_shapes=[pltpu.VMEM((2 * slots, width), F32)],
        compiler_params=params(),
        cost_estimate=cost(2e7, 8e6),
        name="resid_grads",
    )(own, nb, table, gain)


def copy_kernel(ids_ref, in_ref, out_ref):
    out_ref[...] = in_ref[...]


def pick_columns(preact, chip, core, half, rows):
    tokens = preact.shape[0]
    if rows % 128:
        view = preact.reshape(tokens, half, 2, rows)
        view = jnp.take(view, jnp.arange(half) ^ chip, axis=1)
        view = lax.dynamic_index_in_dim(view, core, axis=2, keepdims=False)
        return view.reshape(tokens, half * rows)
    return pl.pallas_call(
        copy_kernel,
        grid_spec=pltpu.PrefetchScalarGridSpec(
            num_scalar_prefetch=1,
            grid=(half,),
            in_specs=[pl.BlockSpec((tokens, rows), lambda j, ids: (0, (ids[0] ^ j) * 2 + ids[1]))],
            out_specs=pl.BlockSpec((tokens, rows), lambda j, ids: (0, j)),
        ),
        out_shape=jax.ShapeDtypeStruct((tokens, half * rows), preact.dtype),
        compiler_params=params(),
        cost_estimate=cost(0, 2e6),
        name="pick_columns",
    )(jnp.stack([chip, core]), preact)


def gelu_kernel(own_ref, nb_ref, act_ref, slope_ref):
    for k, src in enumerate((own_ref, nb_ref)):
        z = src[...].astype(F32)
        cdf = 0.5 * (1.0 + lax.erf(z * 0.7071067811865476))
        density = jnp.exp(-0.5 * z * z) * 0.3989422804014327
        act_ref[k] = (z * cdf).astype(BF)
        slope_ref[k] = cdf + z * density


def gelu(own, nb):
    tokens, units = own.shape
    block = 128
    return pl.pallas_call(
        gelu_kernel,
        grid=(units // block,),
        in_specs=[pl.BlockSpec((tokens, block), lambda j: (0, j))] * 2,
        out_specs=[pl.BlockSpec((2, tokens, block), lambda j: (0, 0, j))] * 2,
        out_shape=(
            jax.ShapeDtypeStruct((2, tokens, units), BF),
            jax.ShapeDtypeStruct((2, tokens, units), F32),
        ),
        compiler_params=params(),
        cost_estimate=cost(6e7, 8e6),
        name="gelu",
    )(own, nb)


def grad_out_kernel(act_ref, resid_ref, out_ref):
    out_ref[...] = lax.dot_general(
        act_ref[...], resid_ref[...], (((0,), (0,)), ((), ())), preferred_element_type=F32
    ).astype(BF)


def grad_out_part(act, resid):
    tokens, units = act.shape
    width = resid.shape[1]
    block = 256
    return pl.pallas_call(
        grad_out_kernel,
        grid=(units // block,),
        in_specs=[
            pl.BlockSpec((tokens, block), lambda j: (0, j)),
            pl.BlockSpec((tokens, width), lambda j: (0, 0)),
        ],
        out_specs=pl.BlockSpec((block, width), lambda j: (j, 0)),
        out_shape=jax.ShapeDtypeStruct((units, width), BF),
        compiler_params=params(),
        cost_estimate=cost(2 * tokens * units * width, 6e6),
        name="grad_out",
    )(act, resid)


def grad_in_kernel(resid_ref, w_ref, slope_ref, own_ref, nb_ref, pre_ref, out_ref):
    tokens = own_ref.shape[0]
    hidden = lax.dot_general(
        resid_ref[...], w_ref[...], (((1,), (1,)), ((), ())), preferred_element_type=F32
    )
    pre = (hidden * slope_ref[...]).astype(BF)
    pre_ref[...] = pre
    contract = (((0,), (0,)), ((), ()))
    out = lax.dot_general(pre[:tokens], own_ref[...], contract, preferred_element_type=F32)
    out = out + lax.dot_general(pre[tokens:], nb_ref[...], contract, preferred_element_type=F32)
    out_ref[...] = out.astype(BF)


def grad_in_part(resid, w_out, slope, states, states_nb):
    tokens, width = resid.shape
    units = w_out.shape[0]
    block = 256
    whole = lambda j: (0, 0)
    return pl.pallas_call(
        grad_in_kernel,
        grid=(units // block,),
        in_specs=[
            pl.BlockSpec((tokens, width), whole),
            pl.BlockSpec((block, width), lambda j: (j, 0)),
            pl.BlockSpec((tokens, block), lambda j: (0, j)),
            pl.BlockSpec(states.shape, whole),
            pl.BlockSpec(states.shape, whole),
        ],
        out_specs=(
            pl.BlockSpec((tokens, block), lambda j: (0, j)),
            pl.BlockSpec((block, width), lambda j: (j, 0)),
        ),
        out_shape=(
            jax.ShapeDtypeStruct((tokens, units), BF),
            jax.ShapeDtypeStruct((units, width), BF),
        ),
        compiler_params=params(),
        cost_estimate=cost(4 * tokens * units * width, 14e6),
        name="grad_in",
    )(resid, w_out, slope, states, states_nb)


def input_nb_kernel(pre_ref, w_ref, out_ref):
    out_ref[...] = jnp.dot(pre_ref[0], w_ref[...], preferred_element_type=F32).astype(BF)


def input_own_kernel(pre_ref, w_ref, resid_ref, nb_ref, out_ref):
    total = jnp.dot(pre_ref[0], w_ref[...], preferred_element_type=F32)
    out_ref[...] = (total + nb_ref[...].astype(F32) + resid_ref[...]).astype(BF)


def input_part(pre, w_in, which, extra):
    _, tokens, units = pre.shape
    width = w_in.shape[1]
    block = 256
    row = pl.BlockSpec((block, width), lambda i: (i, 0))
    return pl.pallas_call(
        input_own_kernel if extra else input_nb_kernel,
        grid=(tokens // block,),
        in_specs=[
            pl.BlockSpec((1, block, units), lambda i: (which, i, 0)),
            pl.BlockSpec((units, width), lambda i: (0, 0)),
        ]
        + [row] * len(extra),
        out_specs=row,
        out_shape=jax.ShapeDtypeStruct((tokens, width), BF),
        compiler_params=params(),
        cost_estimate=cost(2 * tokens * units * width, 5e6),
        name="input_own" if extra else "input_nb",
    )(pre, w_in, *extra)


def gather(x, order):
    done = []
    for mask in order:
        pos = sum(1 for other in done if other > mask)
        x = jnp.stack([x, swap(x, mask)], axis=pos)
        done.append(mask)
    return x


def reduce_step(x, mask, left, last):
    pos = sum(1 for other in left if other > mask)
    keep = lax.index_in_dim(x, 0, pos, keepdims=False)
    send = lax.index_in_dim(x, 1, pos, keepdims=False)
    total = keep.astype(F32) + swap(send, mask).astype(F32)
    return total if last else total.astype(BF)


def reduce_scatter(x, order):
    left = list(order)
    for mask in order:
        x = reduce_step(x, mask, left, mask == order[-1])
        left.remove(mask)
    return x


def shards(
    passage_states,
    saved_preact,
    saved_resid,
    w_in,
    w_out,
    norm_gain,
    query_emb,
    score_grads,
    retrieved,
    placement_map,
    live_counts,
):
    n = lax.axis_size("psg")
    me = lax.axis_index("psg").astype(jnp.int32)
    core, chip = me % 2, me // 2
    half = n // 2
    tokens, width = saved_resid.shape
    rows = w_in.shape[0]
    slots = tokens // LEN
    queries = query_emb.shape[0]
    masks = [1 << b for b in range(1, n.bit_length() - 1)]
    gain = norm_gain.reshape(1, width)
    split = width // 2

    gather_orders = (masks[::-1], masks[:1] + masks[:0:-1])
    reduce_orders = (masks, masks[1::-1] + masks[2:])

    table = pack(
        slots, me.reshape(1), placement_map, live_counts, saved_resid, gain, query_emb, score_grads, retrieved
    )
    mask = 1
    while mask < n:
        table = jnp.concatenate([table, swap(table, mask)], axis=0)
        mask *= 2

    def gather_weight(w):
        parts = [
            gather(w[:, a:b], order)
            for (a, b), order in zip(((0, split), (split, width)), gather_orders)
        ]
        return jnp.concatenate(parts, axis=-1).reshape(half * rows, width)

    out_all = gather_weight(w_out)
    in_all = gather_weight(w_in)

    resid_nb = swap(saved_resid, 1)
    preact_nb = swap(pick_columns(saved_preact, chip, 1 - core, half, rows), 1)
    preact_own = pick_columns(saved_preact, chip, core, half, rows)
    states_nb = swap(passage_states, 1)
    act, slope = gelu(preact_own, preact_nb)

    resid_bf, resid_full, question_grad = resid_grads(slots, queries, saved_resid, resid_nb, table, gain)
    units = half * rows
    resid_bf = resid_bf.reshape(2 * tokens, width)

    def scatter(part):
        part = part.reshape([2] * len(masks) + [rows, width])
        done = [
            reduce_scatter(part[..., a:b], order)
            for (a, b), order in zip(((0, split), (split, width)), reduce_orders)
        ]
        return jnp.concatenate(done, axis=-1)

    grad_out = scatter(grad_out_part(act.reshape(2 * tokens, units), resid_bf))
    pre, in_part = grad_in_part(
        resid_bf, out_all, slope.reshape(2 * tokens, units), passage_states, states_nb
    )
    grad_in = scatter(in_part)
    pre = pre.reshape(2, tokens, units)
    back = swap(input_part(pre, in_all, 1, ()), 1)
    input_grad = input_part(pre, in_all, 0, (resid_full, back))
    return (input_grad, grad_in, grad_out, question_grad)


def solution(mesh):
    both = P(("groups", "psg"), None)
    return jax.shard_map(
        shards,
        mesh=mesh,
        in_specs=(both, both, both, P("psg", None), P("psg", None), P(), both, both, both, P("groups"), P("groups")),
        out_specs=(both, both, both, both),
        check_vma=False,
    )
```

```python
import functools

import jax
import jax.numpy as jnp
from jax import lax
from jax.experimental import pallas as pl
from jax.experimental.pallas import tpu as pltpu
from jax.sharding import PartitionSpec as P

LEN = 128
TICK = 100_000_000
BF = jnp.bfloat16
F32 = jnp.float32
PACK_MIB = 63


def params(mib):
    return pltpu.CompilerParams(vmem_limit_bytes=mib << 20)


FREE = pl.CostEstimate(flops=0, bytes_accessed=0, transcendentals=0)


def swap(x, mask):
    n = lax.axis_size("psg")
    return lax.ppermute(x, "psg", [(i, i ^ mask) for i in range(n)])


def pack_kernel(
    slots, ids_ref, place_in, live_in, resid_in, gain_in, query_in, score_in, ret_in, out_ref,
    place_ref, live_ref, resid_ref, gain_ref, query_ref, score_ref, ret_ref, sems,
):
    me = ids_ref[0]
    passages = place_ref.shape[0]
    width = out_ref.shape[1]
    queries, picks = ret_ref.shape
    inputs = (resid_in, place_in, live_in, ret_in, score_in, query_in, gain_in)
    targets = (resid_ref, place_ref, live_ref, ret_ref, score_ref, query_ref, gain_ref)
    small = [pltpu.make_async_copy(a, b, sems.at[i]) for i, (a, b) in enumerate(zip(inputs, targets))]
    for copy in small:
        copy.start()
    for copy in small[1:]:
        copy.wait()
    ids = ret_ref[...]

    def look(i, placed):
        p = place_ref[i]
        owner = p // slots
        slot = p % slots
        rel = (owner ^ me) * slots + slot
        rel = jnp.where(slot < live_ref[owner], rel, -1)
        return jnp.where(ids == i, rel, placed)

    placed = lax.fori_loop(0, passages, look, jnp.full(ids.shape, -1, jnp.int32), unroll=8)
    score = score_ref[...].astype(F32)
    lanes = max(passages, 128)
    cols = lax.broadcasted_iota(jnp.int32, (queries, lanes), 1)
    pairs = jnp.zeros((queries, lanes), F32)
    for k in range(picks):
        pairs = pairs + jnp.where(cols == placed[:, k : k + 1], score[:, k : k + 1], 0.0)
    if lanes < width:
        pairs = jnp.concatenate([pairs, jnp.zeros((queries, width - lanes), F32)], axis=1)
    small[0].wait()
    rows = []
    for s in range(slots):
        x = resid_ref[s * LEN : (s + 1) * LEN, :].astype(F32)
        centre = x - jnp.mean(x, axis=-1, keepdims=True)
        inverse = lax.rsqrt(jnp.mean(centre * centre, axis=-1, keepdims=True) + 1e-06)
        rows.append(jnp.mean(centre * inverse, axis=0, keepdims=True) * gain_ref[...])
    out_ref[...] = jnp.concatenate(rows + [query_ref[...].astype(F32), pairs], axis=0).astype(BF)


def pack(slots, ids, placement, live, resid, gain, query, score, retrieved):
    width = resid.shape[1]
    queries = query.shape[0]
    smem = pl.BlockSpec(memory_space=pltpu.SMEM)
    hbm = pl.BlockSpec(memory_space=pltpu.HBM)
    scratch = [pltpu.SMEM(x.shape, x.dtype) for x in (placement, live)]
    scratch += [pltpu.VMEM(x.shape, x.dtype) for x in (resid, gain, query, score, retrieved)]
    return pl.pallas_call(
        functools.partial(pack_kernel, slots),
        out_shape=jax.ShapeDtypeStruct((slots + 2 * queries, width), BF),
        in_specs=[smem] + [hbm] * 7,
        out_specs=pl.BlockSpec(memory_space=pltpu.VMEM),
        scratch_shapes=scratch + [pltpu.SemaphoreType.DMA((7,))],
        compiler_params=params(PACK_MIB),
        cost_estimate=FREE,
        name="pack",
    )(ids, placement, live, resid, gain, query, score, retrieved)


def resid_kernel(slots, queries, own_ref, nb_ref, all_ref, gain_ref, bf_ref, question_ref, pass_ref):
    step = pl.program_id(0)
    rows = slots + 2 * queries
    total = all_ref.shape[0]
    lanes = max(total // rows * slots, 128)

    @pl.when(step == 0)
    def _():
        table = all_ref[...]
        head = all_ref[:, :lanes].astype(F32)
        r = lax.broadcasted_iota(jnp.int32, (total, lanes), 0)
        c = lax.broadcasted_iota(jnp.int32, (total, lanes), 1)
        inside = r % rows
        moved = pltpu.roll(head, total - queries, 0)
        is_query = (inside >= slots) & (inside < slots + queries)
        fc = lax.broadcasted_iota(jnp.int32, (lanes, 128), 0)
        fs = lax.broadcasted_iota(jnp.int32, (lanes, 128), 1)
        picked = jnp.zeros((total, 128), F32)
        for k in range(2):
            mine = jnp.where(is_query & (c // slots == ((r // rows) ^ k)), moved, 0.0).astype(BF)
            fold = ((fc % slots + k * slots) == fs).astype(F32).astype(BF)
            picked = picked + jnp.dot(mine, fold, preferred_element_type=F32)
        grads = lax.dot_general(
            picked.astype(BF), table, (((0,), (0,)), ((), ())), preferred_element_type=F32
        )
        pass_ref[...] = grads[: 2 * slots] * gain_ref[...] * (1.0 / LEN)
        own = head[:rows]
        ec = lax.broadcasted_iota(jnp.int32, (lanes, total), 0)
        er = lax.broadcasted_iota(jnp.int32, (lanes, total), 1)
        spread = ((er // rows == ec // slots) & (er % rows == ec % slots)).astype(F32).astype(BF)
        weights = jnp.dot(own.astype(BF), spread, preferred_element_type=F32).astype(BF)
        result = jnp.dot(weights, table, preferred_element_type=F32)
        question_ref[...] = result[slots + queries :]

    for k, src in enumerate((own_ref, nb_ref)):
        x = src[...].astype(F32)
        centre = x - jnp.mean(x, axis=-1, keepdims=True)
        inverse = lax.rsqrt(jnp.mean(centre * centre, axis=-1, keepdims=True) + 1e-06)
        normed = centre * inverse
        scaled = pass_ref[pl.ds(k * slots + step, 1), :]
        base = scaled - jnp.mean(scaled, axis=-1, keepdims=True)
        grad = inverse * (base - normed * jnp.mean(scaled * normed, axis=-1, keepdims=True))
        bf_ref[k] = grad.astype(BF)


def resid_grads(slots, queries, own, nb, table, gain):
    tokens, width = own.shape
    total = table.shape[0]
    return pl.pallas_call(
        functools.partial(resid_kernel, slots, queries),
        grid=(slots,),
        out_shape=(
            jax.ShapeDtypeStruct((2, tokens, width), BF),
            jax.ShapeDtypeStruct((queries, width), F32),
        ),
        in_specs=[
            pl.BlockSpec((LEN, width), lambda s: (s, 0)),
            pl.BlockSpec((LEN, width), lambda s: (s, 0)),
            pl.BlockSpec((total, width), lambda s: (0, 0)),
            pl.BlockSpec((1, width), lambda s: (0, 0)),
        ],
        out_specs=(
            pl.BlockSpec((2, LEN, width), lambda s: (0, s, 0)),
            pl.BlockSpec((queries, width), lambda s: (0, 0)),
        ),
        scratch_shapes=[pltpu.VMEM((2 * slots, width), F32)],
        compiler_params=params(8),
        cost_estimate=FREE,
        name="resid_grads",
    )(own, nb, table, gain)


def gelu_kernel(half, ids_ref, in_ref, act0, act1, slope0, slope1):
    chip, core, group = ids_ref[0] // 2, ids_ref[0] % 2, ids_ref[1]
    width = act0.shape[1]
    for i in range(width // 128):
        if half:
            rows = 2 * width // half
            a, b = (
                in_ref[:, pl.ds(pl.multiple_of(((chip ^ j) * 2 + core) * rows, 128), 128)].astype(F32)
                for j in (2 * i, 2 * i + 1)
            )
            low = jnp.concatenate([a[:, :64], b[:, :64]], axis=1)
            high = jnp.concatenate([a[:, 64:], b[:, 64:]], axis=1)
        else:
            low = in_ref[:, i * 128 : (i + 1) * 128].astype(F32)
            high = in_ref[:, width + i * 128 : width + (i + 1) * 128].astype(F32)
        pair = jnp.where(group == 0, low, high), jnp.where(group == 0, high, low)
        for z, act, slope in zip(pair, (act0, act1), (slope0, slope1)):
            cdf = 0.5 * (1.0 + lax.erf(z * 0.7071067811865476))
            density = jnp.exp(-0.5 * z * z) * 0.3989422804014327
            act[:, i * 128 : (i + 1) * 128] = (z * cdf).astype(BF)
            slope[:, i * 128 : (i + 1) * 128] = cdf + z * density


def gelu(ids, preact, units, half):
    tokens, width = preact.shape
    block = 128
    out = pl.BlockSpec((block, units // 2), lambda i, ids: (i, 0))
    return pl.pallas_call(
        functools.partial(gelu_kernel, half),
        grid_spec=pltpu.PrefetchScalarGridSpec(
            num_scalar_prefetch=1,
            grid=(tokens // block,),
            in_specs=[pl.BlockSpec((block, width), lambda i, ids: (i, 0))],
            out_specs=[out] * 4,
        ),
        out_shape=[jax.ShapeDtypeStruct((tokens, units // 2), t) for t in (BF, BF, F32, F32)],
        compiler_params=params(8),
        cost_estimate=FREE,
        name="gelu",
    )(ids, preact)


def grad_out_kernel(rows, own_ref, nb_ref, resid_ref, keep_ref, sent_ref):
    contract = (((0,), (0,)), ((), ()))
    out = lax.dot_general(own_ref[...], resid_ref[0], contract, preferred_element_type=F32)
    out = out + lax.dot_general(nb_ref[...], resid_ref[1], contract, preferred_element_type=F32)
    keep_ref[...], sent_ref[...] = halves(out, rows)


def grad_out_part(rows, own, nb, resid):
    tokens, units = own.shape
    width = resid.shape[2]
    block = 256
    return pl.pallas_call(
        functools.partial(grad_out_kernel, rows),
        grid=(units // block,),
        in_specs=[pl.BlockSpec((tokens, block), lambda j: (0, j))] * 2
        + [pl.BlockSpec((2, tokens, width), lambda j: (0, 0, 0))],
        out_specs=[pl.BlockSpec((block // 2, width), lambda j: (j, 0))] * 2,
        out_shape=[jax.ShapeDtypeStruct((units // 2, width), BF)] * 2,
        compiler_params=params(12),
        cost_estimate=FREE,
        name="grad_out",
    )(own, nb, resid)


def grad_in_kernel(
    rows, resid_ref, w_ref, slope_own, slope_nb, own_ref, nb_ref, pre_ref, keep_ref, sent_ref
):
    total = None
    for k, (slope, states) in enumerate(((slope_own, own_ref), (slope_nb, nb_ref))):
        hidden = lax.dot_general(
            resid_ref[k], w_ref[...], (((1,), (1,)), ((), ())), preferred_element_type=F32
        )
        pre = (hidden * slope[...]).astype(BF)
        pre_ref[k] = pre
        out = lax.dot_general(
            pre, states[...], (((0,), (0,)), ((), ())), preferred_element_type=F32
        )
        total = out if total is None else total + out
    keep_ref[...], sent_ref[...] = halves(total, rows)


def grad_in_part(rows, resid, w_out, slope_own, slope_nb, states, states_nb):
    _, tokens, width = resid.shape
    units = w_out.shape[0]
    block = 256
    whole = lambda j: (0, 0)
    return pl.pallas_call(
        functools.partial(grad_in_kernel, rows),
        grid=(units // block,),
        in_specs=[
            pl.BlockSpec((2, tokens, width), lambda j: (0, 0, 0)),
            pl.BlockSpec((block, width), lambda j: (j, 0)),
            pl.BlockSpec((tokens, block), lambda j: (0, j)),
            pl.BlockSpec((tokens, block), lambda j: (0, j)),
            pl.BlockSpec(states.shape, whole),
            pl.BlockSpec(states.shape, whole),
        ],
        out_specs=(
            pl.BlockSpec((2, tokens, block), lambda j: (0, 0, j)),
            pl.BlockSpec((block // 2, width), lambda j: (j, 0)),
            pl.BlockSpec((block // 2, width), lambda j: (j, 0)),
        ),
        out_shape=(
            jax.ShapeDtypeStruct((2, tokens, units), BF),
            jax.ShapeDtypeStruct((units // 2, width), BF),
            jax.ShapeDtypeStruct((units // 2, width), BF),
        ),
        compiler_params=params(18),
        cost_estimate=FREE,
        name="grad_in",
    )(resid, w_out, slope_own, slope_nb, states, states_nb)


def input_nb_kernel(pre0, pre1, w0, w1, out_ref):
    total = jnp.dot(pre0[0], w0[...], preferred_element_type=F32)
    total = total + jnp.dot(pre1[0], w1[...], preferred_element_type=F32)
    out_ref[...] = total.astype(BF)


def input_own_kernel(pre0, pre1, w0, w1, resid_ref, nb_ref, mark_ref, out_ref):
    total = jnp.dot(pre0[0], w0[...], preferred_element_type=F32)
    total = total + jnp.dot(pre1[0], w1[...], preferred_element_type=F32)
    out_ref[...] = (total + nb_ref[...].astype(F32) + resid_ref[0].astype(F32)).astype(BF)


def input_part(pre, w_in, which, extra):
    _, tokens, units = pre[0].shape
    width = w_in[0].shape[1]
    block = 256
    row = pl.BlockSpec((block, width), lambda i: (i, 0))
    first = pl.BlockSpec((1, block, width), lambda i: (0, i, 0))
    return pl.pallas_call(
        input_own_kernel if extra else input_nb_kernel,
        grid=(tokens // block,),
        in_specs=[pl.BlockSpec((1, block, units), lambda i: (which, i, 0))] * 2
        + [pl.BlockSpec((units, width), lambda i: (0, 0))] * 2
        + [first, row, pl.BlockSpec(memory_space=pl.ANY)][: len(extra)],
        out_specs=row,
        out_shape=jax.ShapeDtypeStruct((tokens, width), BF),
        compiler_params=params(14),
        cost_estimate=FREE,
        name="input_own" if extra else "input_nb",
    )(*pre, *w_in, *extra)


def tick_kernel(in_ref, out_ref):
    out_ref[...] = in_ref[...]


def tick(x, count):
    vmem = pl.BlockSpec(memory_space=pltpu.VMEM)
    return pl.pallas_call(
        tick_kernel,
        in_specs=[vmem],
        out_specs=vmem,
        out_shape=jax.ShapeDtypeStruct(x.shape, x.dtype),
        compiler_params=params(1),
        cost_estimate=pl.CostEstimate(flops=count * TICK, bytes_accessed=0, transcendentals=0),
        name="tick",
    )(x)


class Order:
    def __init__(self, mark):
        self.mark = mark

    def gate(self, *args):
        *args, self.mark = lax.optimization_barrier((*args, self.mark))
        return args

    def __call__(self, work, *args, ticks=1):
        out = work(*self.gate(*args))
        leaves, tree = jax.tree.flatten(out)
        out = jax.tree.unflatten(tree, self.gate(*leaves))
        if ticks:
            self.mark = tick(self.mark, ticks)
        return out


def place(mask, masks):
    return sum(1 for other in masks if other > mask)


def run(kernel, name, shapes, *args):
    vmem = pl.BlockSpec(memory_space=pltpu.VMEM)
    return pl.pallas_call(
        kernel,
        in_specs=[vmem] * len(args),
        out_specs=[vmem] * len(shapes),
        out_shape=[jax.ShapeDtypeStruct(s, BF) for s in shapes],
        compiler_params=params(6),
        cost_estimate=FREE,
        name=name,
    )(*args)


def join_kernel(rows, a_ref, b_ref, out_ref):
    total, width = a_ref.shape
    if rows % 16:
        a, b = (x[...].astype(F32).reshape(total // rows, rows, width) for x in (a_ref, b_ref))
        out_ref[...] = jnp.stack([a, b], axis=1).reshape(2 * total, width).astype(BF)
        return
    for i in range(total // rows):
        part = slice(i * rows, (i + 1) * rows)
        out_ref[2 * i * rows : (2 * i + 1) * rows] = a_ref[part]
        out_ref[(2 * i + 1) * rows : (2 * i + 2) * rows] = b_ref[part]


def join(a, b, rows):
    total, width = a.shape
    return run(functools.partial(join_kernel, rows), "join", [(2 * total, width)], a, b)[0]


def halves(x, rows):
    total, width = x.shape
    x = x.reshape(total // (2 * rows), 2, rows, width)
    return [x[:, k].reshape(total // 2, width).astype(BF) for k in range(2)]


def fold_kernel(rows, a_ref, b_ref, keep_ref, sent_ref):
    total = a_ref[...].astype(F32) + b_ref[...].astype(F32)
    keep_ref[...], sent_ref[...] = halves(total, rows)


def fold(a, b, rows):
    total, width = a.shape
    return run(functools.partial(fold_kernel, rows), "fold", [(total // 2, width)] * 2, a, b)


def merge_kernel(rows, a0, b0, a1, b1, keep_ref, sent_ref):
    for k, (a, b) in enumerate(((a0, b0), (a1, b1))):
        count = a.shape[0] // 2
        part = slice(k * count, (k + 1) * count)
        keep_ref[part], sent_ref[part] = halves(a[...].astype(F32) + b[...].astype(F32), rows)


def merge(a0, b0, a1, b1, rows):
    total, width = a0.shape
    return run(functools.partial(merge_kernel, rows), "merge", [(total, width)] * 2, a0, b0, a1, b1)


def total_kernel(ids_ref, *refs):
    *parts, mark_ref, out_ref = refs
    rows = out_ref.shape[0] // 2
    sums = [a[...].astype(F32) + b[...].astype(F32) for a, b in zip(parts[::2], parts[1::2])]
    if len(sums) == 1:
        sums = [sums[0][:rows], sums[0][rows:]]
    for k, x in enumerate(sums):
        start = k * rows + (1 - 2 * k) * ids_ref[1] * rows
        out_ref[pl.ds(pl.multiple_of(start, rows), rows)] = x


def total(ids, mark, *chains):
    parts = [x for chain in chains for x in (chain.keep, chain.came)]
    rows = sum(chain.keep.shape[0] for chain in chains)
    vmem = pl.BlockSpec(memory_space=pltpu.VMEM)
    return pl.pallas_call(
        total_kernel,
        in_specs=[pl.BlockSpec(memory_space=pltpu.SMEM)] + [vmem] * (len(parts) + 1),
        out_shape=jax.ShapeDtypeStruct((rows, parts[0].shape[1]), F32),
        compiler_params=params(6),
        cost_estimate=FREE,
        name="total",
    )(ids, *parts, mark)


class Gather:
    def __init__(self, order, x, masks):
        self.order, self.x, self.todo, self.done = order, x, list(masks), []
        self.rows = x.shape[0]

    def send(self):
        if self.todo:
            self.came = swap(*self.order.gate(self.x), self.todo[0])

    def block(self, mask):
        return self.rows << (len(self.done) - place(mask, self.done))

    def step(self, send=True, ticks=1):
        mask = self.todo.pop(0)
        rows = self.block(mask)
        self.x = self.order(lambda a, b: join(a, b, rows), self.x, self.came, ticks=ticks)
        self.done.append(mask)
        self.arrived = self.came
        if send:
            self.send()

    def until(self, left, send=True, ticks=1):
        while len(self.todo) > left:
            self.step(send or len(self.todo) > left + 1, ticks)


class Scatter:
    def __init__(self, order, make, rows, masks):
        self.order, self.make, self.rows, self.left = order, make, rows, list(masks)

    def block(self):
        return self.rows << (len(self.left) - 1 - place(self.left[0], self.left))

    def start(self, *args, send=True):
        rows = self.block()
        *extra, self.keep, self.sent = self.order(lambda *x: self.make(rows, *x), *args, ticks=0)
        if send:
            self.send()
        return extra

    def send(self):
        self.came = swap(*self.order.gate(self.sent), self.left[0])

    def step(self):
        self.left.pop(0)
        rows = self.block()
        self.keep, self.sent = self.order(lambda a, b: fold(a, b, rows), self.keep, self.came)
        self.send()

    def absorb(self, other):
        self.left.pop(0)
        rows = self.block()
        self.keep, self.sent = self.order(
            lambda *x: merge(*x, rows), self.keep, self.came, other.keep, other.came
        )
        self.send()

    def until(self, left):
        while len(self.left) > left:
            self.step()


def shards(
    passage_states,
    saved_preact,
    saved_resid,
    w_in,
    w_out,
    norm_gain,
    query_emb,
    score_grads,
    retrieved,
    placement_map,
    live_counts,
):
    n = lax.axis_size("psg")
    shared = lax.axis_size("groups") == 2
    me = lax.axis_index("psg").astype(jnp.int32)
    group = lax.axis_index("groups").astype(jnp.int32) if shared else jnp.int32(0)
    ids = jnp.stack([me, group])
    core, chip = me % 2, me // 2
    half = n // 2
    tokens, width = saved_resid.shape
    rows = w_in.shape[0]
    units = half * rows
    slots = tokens // LEN
    queries = query_emb.shape[0]
    masks = [1 << b for b in range(1, n.bit_length() - 1)]
    up, down = masks, masks[::-1]
    side = masks[1::-1] + masks[2:]
    gain = norm_gain.reshape(1, width)
    whole_tiles = rows == 128
    order = Order(jnp.zeros((8, 128), F32) + me.astype(F32))

    def cross(x):
        return lax.ppermute(x, "groups", [(0, 1), (1, 0)])

    preact_own = columns = saved_preact
    if not whole_tiles:
        view = saved_preact.reshape(tokens, half, 2, 2, rows // 2)
        view = jnp.take(view, jnp.arange(half) ^ chip, axis=1).transpose(2, 0, 3, 1, 4)
        view = view.reshape(2, tokens, units)
        preact_own = lax.dynamic_index_in_dim(view, core, axis=0, keepdims=False)
        columns = lax.dynamic_index_in_dim(view, 1 - core, axis=0, keepdims=False)
    mine_out, mine_in = (
        lax.dynamic_slice_in_dim(w, group * (rows // 2), rows // 2, 0) for w in (w_out, w_in)
    )
    out = Gather(order, mine_out, down)
    inp = Gather(order, mine_in, down)
    out.send()
    preact_nb = swap(columns, 1)
    resid_nb = swap(saved_resid, 1)
    states_nb = swap(passage_states, 1)
    table = order(
        lambda *args: pack(slots, ids, *args),
        placement_map, live_counts, saved_resid, gain, query_emb, score_grads, retrieved, ticks=0,
    )

    def core_gelu(x):
        return order(lambda x: gelu(ids, x, units, half if whole_tiles else 0), x, ticks=0)

    small = Gather(order, table, masks[:1] + masks[:0:-1] + [1])
    last = len(down)
    out.until(last - 1)
    small.send()
    own = core_gelu(preact_own)
    inp.send()
    small.until(last)
    small.until(last - 1)
    out.until(1)
    early = cross(out.x)
    small.until(1)
    preact_nb, resid_nb, states_nb = order.gate(preact_nb, resid_nb, states_nb)
    near = core_gelu(preact_nb)
    inp.until(last - 1)
    small.until(0)
    resid_bf, question_grad = order(
        lambda a, b, c: resid_grads(slots, queries, a, b, c, gain),
        saved_resid, resid_nb, small.x, ticks=0,
    )

    side_rows = rows // 2
    go0, go1 = (Scatter(order, grad_out_part, side_rows, side) for _ in range(2))
    gi0 = Scatter(order, grad_in_part, side_rows, up)
    gi1 = Scatter(order, grad_in_part, side_rows, side)
    go0.start(own[0], near[0], resid_bf)
    go1.start(own[1], near[1], resid_bf, send=False)
    inp.until(1, send=False)
    early, = order.gate(early)
    out.until(0)
    late = cross(out.arrived)
    inp.send()
    pre0, = gi0.start(resid_bf, out.x, own[2], near[2], passage_states, states_nb)
    go1.send()
    inp.until(0)
    in0 = inp.x
    in1 = cross(in0)
    joined = out.rows << (len(down) - 1 - place(down[-1], down))
    out1 = order(lambda a, b: join(a, b, joined), early, late)
    pre1, = gi1.start(resid_bf, out1, own[3], near[3], passage_states, states_nb)
    go0.absorb(go1)
    gi0.step()
    gi1.step()
    go0.until(1)
    gi0.until(1)
    gi1.until(1)
    go0.came, = order.gate(go0.came)

    pre = (pre0, pre1)
    sent = order(lambda a, b: input_part(pre, (a, b), 1, ()), in0, in1, ticks=0)
    back = swap(sent, 1)
    grad_out = total(ids, order.mark, go0)
    back, = order.gate(back)
    mark = order.mark
    input_grad = order(lambda x: input_part(pre, (in0, in1), 0, (resid_bf, x, mark)), back, ticks=0)
    gi0.came, gi1.came = order.gate(gi0.came, gi1.came)
    grad_in = total(ids, order.mark, gi0, gi1)
    return (input_grad, grad_in, grad_out, question_grad)


def solution(mesh):
    both = P(("groups", "psg"), None)
    return jax.shard_map(
        shards,
        mesh=mesh,
        in_specs=(both, both, both, P("psg", None), P("psg", None), P(), both, both, both, P("groups"), P("groups")),
        out_specs=(both, both, both, both),
        check_vma=False,
    )
```

```python
import functools

import jax
import jax.numpy as jnp
from jax import lax
from jax.experimental import pallas as pl
from jax.experimental.pallas import tpu as pltpu
from jax.sharding import PartitionSpec as P

LEN = 128
TICK = 100_000_000
SCHEDULE = (
    "inp>", "pre>", "resid>", "states>", "out>", "pack", "out:1", "out>", "resid?", "small>",
    "gelu0", "small:1", "small>", "inp:1", "out:1", "out>", "xa", "ia?", "small:30", "small>",
    "inp>", "gelu1", "small:30", "small>", "states?", "small:1", "resid", "out:1", "xa?", "ib?",
    "xb", "inp:1", "inp>", "gi0", "xa?", "go1", "ia?", "go0", "go0>", "gi0>", "inp:1", "wout",
    "gi1", "go1>", "gi1>", "ia", "go0:1", "go0>", "gi0", "ia?", "gi0>", "ib", "go1:1", "go1>",
    "gi1:1", "gi1>", "go0:1", "gi0", "gi0>", "go0>", "win", "nb0", "go1:1", "go1>", "nb1", "go0?",
    "gi1:30", "gi1>", "gi0?", "nb?", "own", "tgo", "tgi",
)
ORDERS = {"out": "down", "inp": "far", "go0": "side", "go1": "far", "gi0": "up", "gi1": "side"}
BF = jnp.bfloat16
F32 = jnp.float32
PACK_MIB = 63


def params(mib):
    return pltpu.CompilerParams(vmem_limit_bytes=mib << 20)


FREE = pl.CostEstimate(flops=0, bytes_accessed=0, transcendentals=0)


def swap(x, mask):
    n = lax.axis_size("psg")
    return lax.ppermute(x, "psg", [(i, i ^ mask) for i in range(n)])


def pack_kernel(
    slots, ids_ref, place_in, live_in, resid_in, gain_in, query_in, score_in, ret_in, out_ref,
    place_ref, live_ref, resid_ref, gain_ref, query_ref, score_ref, ret_ref, sems,
):
    me = ids_ref[0]
    passages = place_ref.shape[0]
    width = out_ref.shape[1]
    queries, picks = ret_ref.shape
    inputs = (resid_in, place_in, live_in, ret_in, score_in, query_in, gain_in)
    targets = (resid_ref, place_ref, live_ref, ret_ref, score_ref, query_ref, gain_ref)
    small = [pltpu.make_async_copy(a, b, sems.at[i]) for i, (a, b) in enumerate(zip(inputs, targets))]
    for copy in small:
        copy.start()
    for copy in small[1:]:
        copy.wait()
    ids = ret_ref[...]

    def look(i, placed):
        p = place_ref[i]
        owner = p // slots
        slot = p % slots
        rel = (owner ^ me) * slots + slot
        rel = jnp.where(slot < live_ref[owner], rel, -1)
        return jnp.where(ids == i, rel, placed)

    placed = lax.fori_loop(0, passages, look, jnp.full(ids.shape, -1, jnp.int32), unroll=8)
    score = score_ref[...].astype(F32)
    lanes = max(passages, 128)
    cols = lax.broadcasted_iota(jnp.int32, (queries, lanes), 1)
    pairs = jnp.zeros((queries, lanes), F32)
    for k in range(picks):
        pairs = pairs + jnp.where(cols == placed[:, k : k + 1], score[:, k : k + 1], 0.0)
    if lanes < width:
        pairs = jnp.concatenate([pairs, jnp.zeros((queries, width - lanes), F32)], axis=1)
    small[0].wait()
    rows = []
    for s in range(slots):
        x = resid_ref[s * LEN : (s + 1) * LEN, :].astype(F32)
        centre = x - jnp.mean(x, axis=-1, keepdims=True)
        inverse = lax.rsqrt(jnp.mean(centre * centre, axis=-1, keepdims=True) + 1e-06)
        rows.append(jnp.mean(centre * inverse, axis=0, keepdims=True) * gain_ref[...])
    out_ref[...] = jnp.concatenate(rows + [query_ref[...].astype(F32), pairs], axis=0).astype(BF)


def pack(slots, ids, placement, live, resid, gain, query, score, retrieved):
    width = resid.shape[1]
    queries = query.shape[0]
    smem = pl.BlockSpec(memory_space=pltpu.SMEM)
    hbm = pl.BlockSpec(memory_space=pltpu.HBM)
    scratch = [pltpu.SMEM(x.shape, x.dtype) for x in (placement, live)]
    scratch += [pltpu.VMEM(x.shape, x.dtype) for x in (resid, gain, query, score, retrieved)]
    return pl.pallas_call(
        functools.partial(pack_kernel, slots),
        out_shape=jax.ShapeDtypeStruct((slots + 2 * queries, width), BF),
        in_specs=[smem] + [hbm] * 7,
        out_specs=pl.BlockSpec(memory_space=pltpu.VMEM),
        scratch_shapes=scratch + [pltpu.SemaphoreType.DMA((7,))],
        compiler_params=params(PACK_MIB),
        cost_estimate=FREE,
        name="pack",
    )(ids, placement, live, resid, gain, query, score, retrieved)


def resid_kernel(slots, queries, own_ref, nb_ref, all_ref, gain_ref, bf_ref, question_ref, pass_ref):
    step = pl.program_id(0)
    rows = slots + 2 * queries
    total = all_ref.shape[0]
    lanes = max(total // rows * slots, 128)

    @pl.when(step == 0)
    def _():
        table = all_ref[...]
        head = all_ref[:, :lanes].astype(F32)
        r = lax.broadcasted_iota(jnp.int32, (total, lanes), 0)
        c = lax.broadcasted_iota(jnp.int32, (total, lanes), 1)
        inside = r % rows
        moved = pltpu.roll(head, total - queries, 0)
        is_query = (inside >= slots) & (inside < slots + queries)
        fc = lax.broadcasted_iota(jnp.int32, (lanes, 128), 0)
        fs = lax.broadcasted_iota(jnp.int32, (lanes, 128), 1)
        picked = jnp.zeros((total, 128), F32)
        for k in range(2):
            mine = jnp.where(is_query & (c // slots == ((r // rows) ^ k)), moved, 0.0).astype(BF)
            fold = ((fc % slots + k * slots) == fs).astype(F32).astype(BF)
            picked = picked + jnp.dot(mine, fold, preferred_element_type=F32)
        grads = lax.dot_general(
            picked.astype(BF), table, (((0,), (0,)), ((), ())), preferred_element_type=F32
        )
        pass_ref[...] = grads[: 2 * slots] * gain_ref[...] * (1.0 / LEN)
        own = head[:rows]
        ec = lax.broadcasted_iota(jnp.int32, (lanes, total), 0)
        er = lax.broadcasted_iota(jnp.int32, (lanes, total), 1)
        spread = ((er // rows == ec // slots) & (er % rows == ec % slots)).astype(F32).astype(BF)
        weights = jnp.dot(own.astype(BF), spread, preferred_element_type=F32).astype(BF)
        result = jnp.dot(weights, table, preferred_element_type=F32)
        question_ref[...] = result[slots + queries :]

    for k, src in enumerate((own_ref, nb_ref)):
        x = src[...].astype(F32)
        centre = x - jnp.mean(x, axis=-1, keepdims=True)
        inverse = lax.rsqrt(jnp.mean(centre * centre, axis=-1, keepdims=True) + 1e-06)
        normed = centre * inverse
        scaled = pass_ref[pl.ds(k * slots + step, 1), :]
        base = scaled - jnp.mean(scaled, axis=-1, keepdims=True)
        grad = inverse * (base - normed * jnp.mean(scaled * normed, axis=-1, keepdims=True))
        bf_ref[k] = grad.astype(BF)


def resid_grads(slots, queries, own, nb, table, gain):
    tokens, width = own.shape
    total = table.shape[0]
    return pl.pallas_call(
        functools.partial(resid_kernel, slots, queries),
        grid=(slots,),
        out_shape=(
            jax.ShapeDtypeStruct((2, tokens, width), BF),
            jax.ShapeDtypeStruct((queries, width), F32),
        ),
        in_specs=[
            pl.BlockSpec((LEN, width), lambda s: (s, 0)),
            pl.BlockSpec((LEN, width), lambda s: (s, 0)),
            pl.BlockSpec((total, width), lambda s: (0, 0)),
            pl.BlockSpec((1, width), lambda s: (0, 0)),
        ],
        out_specs=(
            pl.BlockSpec((2, LEN, width), lambda s: (0, s, 0)),
            pl.BlockSpec((queries, width), lambda s: (0, 0)),
        ),
        scratch_shapes=[pltpu.VMEM((2 * slots, width), F32)],
        compiler_params=params(8),
        cost_estimate=FREE,
        name="resid_grads",
    )(own, nb, table, gain)


def gelu_kernel(half, ids_ref, in_ref, act0, act1, slope0, slope1):
    chip, core, group = ids_ref[0] // 2, ids_ref[0] % 2, ids_ref[1]
    width = act0.shape[1]
    for i in range(width // 128):
        if half:
            rows = 2 * width // half
            a, b = (
                in_ref[:, pl.ds(pl.multiple_of(((chip ^ j) * 2 + core) * rows, 128), 128)].astype(F32)
                for j in (2 * i, 2 * i + 1)
            )
            low = jnp.concatenate([a[:, :64], b[:, :64]], axis=1)
            high = jnp.concatenate([a[:, 64:], b[:, 64:]], axis=1)
        else:
            low = in_ref[:, i * 128 : (i + 1) * 128].astype(F32)
            high = in_ref[:, width + i * 128 : width + (i + 1) * 128].astype(F32)
        pair = jnp.where(group == 0, low, high), jnp.where(group == 0, high, low)
        for z, act, slope in zip(pair, (act0, act1), (slope0, slope1)):
            cdf = 0.5 * (1.0 + lax.erf(z * 0.7071067811865476))
            density = jnp.exp(-0.5 * z * z) * 0.3989422804014327
            act[:, i * 128 : (i + 1) * 128] = (z * cdf).astype(BF)
            slope[:, i * 128 : (i + 1) * 128] = cdf + z * density


def gelu(ids, preact, units, half):
    tokens, width = preact.shape
    block = 128
    out = pl.BlockSpec((block, units // 2), lambda i, ids: (i, 0))
    return pl.pallas_call(
        functools.partial(gelu_kernel, half),
        grid_spec=pltpu.PrefetchScalarGridSpec(
            num_scalar_prefetch=1,
            grid=(tokens // block,),
            in_specs=[pl.BlockSpec((block, width), lambda i, ids: (i, 0))],
            out_specs=[out] * 4,
        ),
        out_shape=[jax.ShapeDtypeStruct((tokens, units // 2), t) for t in (BF, BF, F32, F32)],
        compiler_params=params(8),
        cost_estimate=FREE,
        name="gelu",
    )(ids, preact)


def grad_out_kernel(rows, own_ref, nb_ref, resid_ref, keep_ref, sent_ref):
    contract = (((0,), (0,)), ((), ()))
    out = lax.dot_general(own_ref[...], resid_ref[0], contract, preferred_element_type=F32)
    out = out + lax.dot_general(nb_ref[...], resid_ref[1], contract, preferred_element_type=F32)
    keep_ref[...], sent_ref[...] = halves(out, rows)


def grad_out_part(rows, own, nb, resid):
    tokens, units = own.shape
    width = resid.shape[2]
    block = 256
    return pl.pallas_call(
        functools.partial(grad_out_kernel, rows),
        grid=(units // block,),
        in_specs=[pl.BlockSpec((tokens, block), lambda j: (0, j))] * 2
        + [pl.BlockSpec((2, tokens, width), lambda j: (0, 0, 0))],
        out_specs=[pl.BlockSpec((block // 2, width), lambda j: (j, 0))] * 2,
        out_shape=[jax.ShapeDtypeStruct((units // 2, width), BF)] * 2,
        compiler_params=params(12),
        cost_estimate=FREE,
        name="grad_out",
    )(own, nb, resid)


def grad_in_kernel(
    rows, resid_ref, w_ref, slope_own, slope_nb, own_ref, nb_ref, pre_ref, keep_ref, sent_ref
):
    total = None
    for k, (slope, states) in enumerate(((slope_own, own_ref), (slope_nb, nb_ref))):
        hidden = lax.dot_general(
            resid_ref[k], w_ref[...], (((1,), (1,)), ((), ())), preferred_element_type=F32
        )
        pre = (hidden * slope[...]).astype(BF)
        pre_ref[k] = pre
        out = lax.dot_general(
            pre, states[...], (((0,), (0,)), ((), ())), preferred_element_type=F32
        )
        total = out if total is None else total + out
    keep_ref[...], sent_ref[...] = halves(total, rows)


def grad_in_part(rows, resid, w_out, slope_own, slope_nb, states, states_nb):
    _, tokens, width = resid.shape
    units = w_out.shape[0]
    block = 256
    whole = lambda j: (0, 0)
    return pl.pallas_call(
        functools.partial(grad_in_kernel, rows),
        grid=(units // block,),
        in_specs=[
            pl.BlockSpec((2, tokens, width), lambda j: (0, 0, 0)),
            pl.BlockSpec((block, width), lambda j: (j, 0)),
            pl.BlockSpec((tokens, block), lambda j: (0, j)),
            pl.BlockSpec((tokens, block), lambda j: (0, j)),
            pl.BlockSpec(states.shape, whole),
            pl.BlockSpec(states.shape, whole),
        ],
        out_specs=(
            pl.BlockSpec((2, tokens, block), lambda j: (0, 0, j)),
            pl.BlockSpec((block // 2, width), lambda j: (j, 0)),
            pl.BlockSpec((block // 2, width), lambda j: (j, 0)),
        ),
        out_shape=(
            jax.ShapeDtypeStruct((2, tokens, units), BF),
            jax.ShapeDtypeStruct((units // 2, width), BF),
            jax.ShapeDtypeStruct((units // 2, width), BF),
        ),
        compiler_params=params(18),
        cost_estimate=FREE,
        name="grad_in",
    )(resid, w_out, slope_own, slope_nb, states, states_nb)


def input_nb_kernel(pre0, pre1, w0, w1, out_ref):
    total = jnp.dot(pre0[0], w0[...], preferred_element_type=F32)
    total = total + jnp.dot(pre1[0], w1[...], preferred_element_type=F32)
    out_ref[...] = total.astype(BF)


def input_own_kernel(pre0, pre1, w0, w1, resid_ref, first_ref, second_ref, mark_ref, out_ref):
    total = jnp.dot(pre0[0], w0[...], preferred_element_type=F32)
    total = total + jnp.dot(pre1[0], w1[...], preferred_element_type=F32)
    total = total + resid_ref[0].astype(F32)

    @pl.when(pl.program_id(0) == 0)
    def _():
        out_ref[...] = (total + first_ref[...].astype(F32)).astype(BF)

    @pl.when(pl.program_id(0) == 1)
    def _():
        out_ref[...] = (total + second_ref[...].astype(F32)).astype(BF)


def input_nb(pre, w_in, part):
    _, tokens, units = pre[0].shape
    width = w_in[0].shape[1]
    block = tokens // 2
    return pl.pallas_call(
        input_nb_kernel,
        grid=(1,),
        in_specs=[pl.BlockSpec((1, block, units), lambda i: (1, part, 0))] * 2
        + [pl.BlockSpec((units, width), lambda i: (0, 0))] * 2,
        out_specs=pl.BlockSpec((block, width), lambda i: (0, 0)),
        out_shape=jax.ShapeDtypeStruct((block, width), BF),
        compiler_params=params(12),
        cost_estimate=FREE,
        name="input_nb",
    )(*pre, *w_in)


def input_own(pre, w_in, resid, first, second, mark):
    _, tokens, units = pre[0].shape
    width = w_in[0].shape[1]
    block = tokens // 2
    whole = lambda i: (0, 0)
    return pl.pallas_call(
        input_own_kernel,
        grid=(2,),
        in_specs=[pl.BlockSpec((1, block, units), lambda i: (0, i, 0))] * 2
        + [pl.BlockSpec((units, width), whole)] * 2
        + [pl.BlockSpec((1, block, width), lambda i: (0, i, 0))]
        + [pl.BlockSpec((block, width), whole)] * 2
        + [pl.BlockSpec(memory_space=pl.ANY)],
        out_specs=pl.BlockSpec((block, width), lambda i: (i, 0)),
        out_shape=jax.ShapeDtypeStruct((tokens, width), BF),
        compiler_params=params(16),
        cost_estimate=FREE,
        name="input_own",
    )(*pre, *w_in, resid, first, second, mark)


def tick_kernel(in_ref, out_ref):
    out_ref[...] = in_ref[...]


def tick(x, count):
    vmem = pl.BlockSpec(memory_space=pltpu.VMEM)
    return pl.pallas_call(
        tick_kernel,
        in_specs=[vmem],
        out_specs=vmem,
        out_shape=jax.ShapeDtypeStruct(x.shape, x.dtype),
        compiler_params=params(1),
        cost_estimate=pl.CostEstimate(flops=count * TICK, bytes_accessed=0, transcendentals=0),
        name="tick",
    )(x)


class Order:
    def __init__(self, mark):
        self.mark = mark

    def gate(self, *args):
        *args, self.mark = lax.optimization_barrier((*args, self.mark))
        return args

    def __call__(self, work, *args, ticks=1):
        out = work(*self.gate(*args))
        leaves, tree = jax.tree.flatten(out)
        out = jax.tree.unflatten(tree, self.gate(*leaves))
        if ticks:
            self.mark = tick(self.mark, ticks)
        return out


def place(mask, masks):
    return sum(1 for other in masks if other > mask)


def run(kernel, name, shapes, *args):
    vmem = pl.BlockSpec(memory_space=pltpu.VMEM)
    return pl.pallas_call(
        kernel,
        in_specs=[vmem] * len(args),
        out_specs=[vmem] * len(shapes),
        out_shape=[jax.ShapeDtypeStruct(s, BF) for s in shapes],
        compiler_params=params(6),
        cost_estimate=FREE,
        name=name,
    )(*args)


def join_kernel(rows, a_ref, b_ref, out_ref):
    total, width = a_ref.shape
    if rows % 16:
        a, b = (x[...].astype(F32).reshape(total // rows, rows, width) for x in (a_ref, b_ref))
        out_ref[...] = jnp.stack([a, b], axis=1).reshape(2 * total, width).astype(BF)
        return
    for i in range(total // rows):
        part = slice(i * rows, (i + 1) * rows)
        out_ref[2 * i * rows : (2 * i + 1) * rows] = a_ref[part]
        out_ref[(2 * i + 1) * rows : (2 * i + 2) * rows] = b_ref[part]


def join(a, b, rows):
    total, width = a.shape
    return run(functools.partial(join_kernel, rows), "join", [(2 * total, width)], a, b)[0]


def halves(x, rows):
    total, width = x.shape
    x = x.reshape(total // (2 * rows), 2, rows, width)
    return [x[:, k].reshape(total // 2, width).astype(BF) for k in range(2)]


def fold_kernel(rows, a_ref, b_ref, keep_ref, sent_ref):
    total = a_ref[...].astype(F32) + b_ref[...].astype(F32)
    keep_ref[...], sent_ref[...] = halves(total, rows)


def fold(a, b, rows):
    total, width = a.shape
    return run(functools.partial(fold_kernel, rows), "fold", [(total // 2, width)] * 2, a, b)


def total_kernel(ids_ref, *refs):
    *parts, mark_ref, out_ref = refs
    rows = out_ref.shape[0] // 2
    sums = [a[...].astype(F32) + b[...].astype(F32) for a, b in zip(parts[::2], parts[1::2])]
    if len(sums) == 1:
        sums = [sums[0][:rows], sums[0][rows:]]
    for k, x in enumerate(sums):
        start = k * rows + (1 - 2 * k) * ids_ref[1] * rows
        out_ref[pl.ds(pl.multiple_of(start, rows), rows)] = x


def total(ids, mark, *chains):
    parts = [x for chain in chains for x in (chain.keep, chain.came)]
    rows = sum(chain.keep.shape[0] for chain in chains)
    vmem = pl.BlockSpec(memory_space=pltpu.VMEM)
    return pl.pallas_call(
        total_kernel,
        in_specs=[pl.BlockSpec(memory_space=pltpu.SMEM)] + [vmem] * (len(parts) + 1),
        out_shape=jax.ShapeDtypeStruct((rows, parts[0].shape[1]), F32),
        compiler_params=params(6),
        cost_estimate=FREE,
        name="total",
    )(ids, *parts, mark)


class Chain:
    def __init__(self, order, masks, rows):
        self.order, self.left, self.done, self.rows = order, list(masks), [], rows
        self.steps = 3

    def due(self, last):
        self.steps -= 1
        while len(self.left) > max(self.steps, last):
            yield self.left[0]


class Gather(Chain):
    def __init__(self, order, x, masks):
        super().__init__(order, masks, x.shape[0])
        self.x = x
        self.steps = min(len(self.left), 4 if masks[-1] == 1 else 3)

    def send(self):
        self.came = swap(*self.order.gate(self.x), self.left[0])

    def step(self, ticks):
        first = True
        for mask in self.due(0):
            if not first:
                self.send()
            first = False
            rows = self.rows << (len(self.done) - place(mask, self.done))
            self.before, self.arrived, self.block = self.x, self.came, rows
            self.x = self.order(lambda a, b: join(a, b, rows), self.x, self.came, ticks=ticks)
            self.done.append(self.left.pop(0))


class Scatter(Chain):
    def block(self):
        return self.rows << (len(self.left) - 1 - place(self.left[0], self.left))

    def start(self, make, *args):
        rows = self.block()
        *extra, self.keep, self.sent = self.order(lambda *x: make(rows, *x), *args, ticks=0)
        return extra

    def send(self):
        self.came = swap(*self.order.gate(self.sent), self.left[0])

    def step(self, ticks):
        first = True
        for _ in self.due(1):
            if not first:
                self.send()
            first = False
            self.left.pop(0)
            rows = self.block()
            self.keep, self.sent = self.order(
                lambda a, b: fold(a, b, rows), self.keep, self.came, ticks=ticks
            )


def shards(
    passage_states,
    saved_preact,
    saved_resid,
    w_in,
    w_out,
    norm_gain,
    query_emb,
    score_grads,
    retrieved,
    placement_map,
    live_counts,
):
    n = lax.axis_size("psg")
    shared = lax.axis_size("groups") == 2
    me = lax.axis_index("psg").astype(jnp.int32)
    group = lax.axis_index("groups").astype(jnp.int32) if shared else jnp.int32(0)
    ids = jnp.stack([me, group])
    core, chip = me % 2, me // 2
    half = n // 2
    tokens, width = saved_resid.shape
    rows = w_in.shape[0]
    units = half * rows
    slots = tokens // LEN
    queries = query_emb.shape[0]
    masks = [1 << b for b in range(1, n.bit_length() - 1)]
    orders = {
        "up": masks,
        "down": masks[::-1],
        "side": masks[1::-1] + masks[2:],
        "far": masks[:1] + masks[:0:-1],
        "mixed": masks[1:2] + masks[:1:-1] + masks[:1],
        "low": masks[:1:-1] + masks[:2],
    }
    gain = norm_gain.reshape(1, width)
    whole_tiles = rows == 128
    order = Order(jnp.zeros((8, 128), F32) + me.astype(F32))

    def cross(x):
        return lax.ppermute(x, "groups", [(0, 1), (1, 0)])

    preact_own = columns = saved_preact
    if not whole_tiles:
        view = saved_preact.reshape(tokens, half, 2, 2, rows // 2)
        view = jnp.take(view, jnp.arange(half) ^ chip, axis=1).transpose(2, 0, 3, 1, 4)
        view = view.reshape(2, tokens, units)
        preact_own = lax.dynamic_index_in_dim(view, core, axis=0, keepdims=False)
        columns = lax.dynamic_index_in_dim(view, 1 - core, axis=0, keepdims=False)
    mine_out, mine_in = (
        lax.dynamic_slice_in_dim(w, group * (rows // 2), rows // 2, 0) for w in (w_out, w_in)
    )
    v, swapped = {}, {"pre": columns, "resid": saved_resid, "states": passage_states}
    chains = {
        "out": Gather(order, mine_out, orders[ORDERS["out"]]),
        "inp": Gather(order, mine_in, orders[ORDERS["inp"]]),
    }
    for name in ("go0", "go1", "gi0", "gi1"):
        chains[name] = Scatter(order, orders[ORDERS[name]], rows // 2)

    def weight(chain, first, second):
        return order(lambda a, b: join(a, b, chain.block), v.pop(first), v.pop(second), ticks=0)

    for word in SCHEDULE:
        name, _, ticks = word.partition(":")
        ticks = int(ticks or 0)
        chain = chains.get(name.rstrip(">"))
        if name[:-1] in swapped and name.endswith(">"):
            x = swapped[name[:-1]]
            v[name[:-1]] = swap(*order.gate(x), 1) if ticks else swap(x, 1)
        elif name.endswith(">"):
            chain.send()
        elif name.endswith("?"):
            if name[:-1] in chains:
                chain = chains[name[:-1]]
                chain.came, = order.gate(chain.came)
            for key in [k for k in v if k.startswith(name[:-1])]:
                v[key], = order.gate(v[key])
            if ticks:
                order.mark = tick(order.mark, ticks)
        elif name in ("out", "inp", "small"):
            chain.step(ticks)
        elif name == "pack":
            table = order(
                lambda *args: pack(slots, ids, *args),
                placement_map, live_counts, saved_resid, gain, query_emb, score_grads, retrieved, ticks=0,
            )
            chains["small"] = Gather(order, table, orders["far"] + [1])
        elif name in ("gelu0", "gelu1"):
            x = preact_own if name == "gelu0" else v["pre"]
            v[name] = order(lambda x: gelu(ids, x, units, half if whole_tiles else 0), x, ticks=0)
        elif name == "resid":
            resid_bf, question_grad = order(
                lambda a, b, c: resid_grads(slots, queries, a, b, c, gain),
                saved_resid, v["resid"], chains["small"].x, ticks=0,
            )
        elif name in ("go0", "go1", "gi0", "gi1"):
            k = int(name[2])
            if chain.steps < 3 or hasattr(chain, "keep"):
                chain.step(ticks)
            elif name[:2] == "go":
                chain.start(grad_out_part, v["gelu0"][k], v["gelu1"][k], resid_bf)
            else:
                v["p%d" % k], = chain.start(
                    grad_in_part, resid_bf, chains["out"].x if k == 0 else out1,
                    v["gelu0"][2 + k], v["gelu1"][2 + k], passage_states, v["states"],
                )
        elif name == "xa":
            v["xa"] = cross(*order.gate(chains["out"].x))
        elif name == "xb":
            v["xb"] = cross(*order.gate(chains["out"].arrived))
        elif name == "ia":
            v["ia"] = cross(*order.gate(chains["inp"].before if chains["inp"].steps == 0 else chains["inp"].x))
        elif name == "ib":
            v["ib"] = cross(*order.gate(chains["inp"].arrived))
        elif name == "wout":
            out1 = weight(chains["out"], "xa", "xb")
        elif name == "win":
            w_in = (chains["inp"].x, weight(chains["inp"], "ia", "ib"))
        elif name in ("nb0", "nb1"):
            k = int(name[2])
            v[name] = swap(order(lambda *w: input_nb((v["p0"], v["p1"]), w, k), *w_in, ticks=0), 1)
        elif name == "own":
            mark = order.mark
            input_grad = order(
                lambda a, b: input_own((v["p0"], v["p1"]), w_in, resid_bf, a, b, mark), v["nb0"], v["nb1"],
                ticks=0,
            )
        elif name in ("tgo", "tgi"):
            pair = [chains[name[1:] + k] for k in "01"]
            pair[0].came, pair[1].came = order.gate(pair[0].came, pair[1].came)
            v[name] = total(ids, order.mark, *pair)
        else:
            raise ValueError(word)
    return (input_grad, v["tgi"], v["tgo"], question_grad)


def solution(mesh):
    both = P(("groups", "psg"), None)
    return jax.shard_map(
        shards,
        mesh=mesh,
        in_specs=(both, both, both, P("psg", None), P("psg", None), P(), both, both, both, P("groups"), P("groups")),
        out_specs=(both, both, both, both),
        check_vma=False,
    )
```

```python
import functools

import jax
import jax.numpy as jnp
from jax import lax
from jax.experimental import pallas as pl
from jax.experimental.pallas import tpu as pltpu
from jax.sharding import PartitionSpec as P

LEN = 128
TICK = 100_000_000
SCHEDULE = (
    "inp>", "pre>", "resid>", "states>", "out>", "pack", "out:30", "out>", "resid?", "small>",
    "gelu0", "small:1", "small>", "inp:1", "out:1", "out>", "xa", "small:30", "small>", "inp>",
    "gelu1", "small:30", "small>", "small:1", "resid", "out:1", "xa?", "xb", "inp:1", "states?",
    "inp>", "gi0", "go1", "xa?", "ia?", "go0", "go0>", "go1>", "gi0>", "inp:1", "wout", "gi1",
    "gi1>", "ia", "go0:1", "go0>", "gi0", "ia?", "gi0>", "ib", "go1:1", "go1>", "go0?", "gi1:1",
    "gi1>", "go0:1", "gi0", "gi0>", "go0>", "win", "nb0", "go1:1", "go1>", "nb1", "go0?", "gi1:30",
    "gi1>", "gi0?", "nb?", "own", "tgo", "tgi",
)
ORDERS = {"out": "down", "inp": "far", "go0": "side", "go1": "far", "gi0": "up", "gi1": "side"}
BF = jnp.bfloat16
F32 = jnp.float32
PACK_MIB = 63


def params(mib):
    return pltpu.CompilerParams(vmem_limit_bytes=mib << 20)


FREE = pl.CostEstimate(flops=0, bytes_accessed=0, transcendentals=0)


def swap(x, mask):
    n = lax.axis_size("psg")
    return lax.ppermute(x, "psg", [(i, i ^ mask) for i in range(n)])


def pack_kernel(
    slots, ids_ref, place_in, live_in, resid_in, gain_in, query_in, score_in, ret_in, out_ref,
    place_ref, live_ref, resid_ref, gain_ref, query_ref, score_ref, ret_ref, sems,
):
    me = ids_ref[0]
    passages = place_ref.shape[0]
    width = out_ref.shape[1]
    queries, picks = ret_ref.shape
    inputs = (resid_in, place_in, live_in, ret_in, score_in, query_in, gain_in)
    targets = (resid_ref, place_ref, live_ref, ret_ref, score_ref, query_ref, gain_ref)
    small = [pltpu.make_async_copy(a, b, sems.at[i]) for i, (a, b) in enumerate(zip(inputs, targets))]
    for copy in small:
        copy.start()
    for copy in small[1:]:
        copy.wait()
    ids = ret_ref[...]

    def look(i, placed):
        p = place_ref[i]
        owner = p // slots
        slot = p % slots
        rel = (owner ^ me) * slots + slot
        rel = jnp.where(slot < live_ref[owner], rel, -1)
        return jnp.where(ids == i, rel, placed)

    placed = lax.fori_loop(0, passages, look, jnp.full(ids.shape, -1, jnp.int32), unroll=8)
    score = score_ref[...].astype(F32)
    lanes = max(passages, 128)
    cols = lax.broadcasted_iota(jnp.int32, (queries, lanes), 1)
    pairs = jnp.zeros((queries, lanes), F32)
    for k in range(picks):
        pairs = pairs + jnp.where(cols == placed[:, k : k + 1], score[:, k : k + 1], 0.0)
    if lanes < width:
        pairs = jnp.concatenate([pairs, jnp.zeros((queries, width - lanes), F32)], axis=1)
    small[0].wait()
    rows = []
    for s in range(slots):
        x = resid_ref[s * LEN : (s + 1) * LEN, :].astype(F32)
        centre = x - jnp.mean(x, axis=-1, keepdims=True)
        inverse = lax.rsqrt(jnp.mean(centre * centre, axis=-1, keepdims=True) + 1e-06)
        rows.append(jnp.mean(centre * inverse, axis=0, keepdims=True) * gain_ref[...])
    out_ref[...] = jnp.concatenate(rows + [query_ref[...].astype(F32), pairs], axis=0).astype(BF)


def pack(slots, ids, placement, live, resid, gain, query, score, retrieved):
    width = resid.shape[1]
    queries = query.shape[0]
    smem = pl.BlockSpec(memory_space=pltpu.SMEM)
    hbm = pl.BlockSpec(memory_space=pltpu.HBM)
    scratch = [pltpu.SMEM(x.shape, x.dtype) for x in (placement, live)]
    scratch += [pltpu.VMEM(x.shape, x.dtype) for x in (resid, gain, query, score, retrieved)]
    return pl.pallas_call(
        functools.partial(pack_kernel, slots),
        out_shape=jax.ShapeDtypeStruct((slots + 2 * queries, width), BF),
        in_specs=[smem] + [hbm] * 7,
        out_specs=pl.BlockSpec(memory_space=pltpu.VMEM),
        scratch_shapes=scratch + [pltpu.SemaphoreType.DMA((7,))],
        compiler_params=params(PACK_MIB),
        cost_estimate=FREE,
        name="pack",
    )(ids, placement, live, resid, gain, query, score, retrieved)


def resid_kernel(slots, queries, own_ref, nb_ref, all_ref, gain_ref, bf_ref, question_ref, pass_ref):
    step = pl.program_id(0)
    rows = slots + 2 * queries
    total = all_ref.shape[0]
    lanes = max(total // rows * slots, 128)

    @pl.when(step == 0)
    def _():
        table = all_ref[...]
        head = all_ref[:, :lanes].astype(F32)
        r = lax.broadcasted_iota(jnp.int32, (total, lanes), 0)
        c = lax.broadcasted_iota(jnp.int32, (total, lanes), 1)
        inside = r % rows
        moved = pltpu.roll(head, total - queries, 0)
        is_query = (inside >= slots) & (inside < slots + queries)
        fc = lax.broadcasted_iota(jnp.int32, (lanes, 128), 0)
        fs = lax.broadcasted_iota(jnp.int32, (lanes, 128), 1)
        picked = jnp.zeros((total, 128), F32)
        for k in range(2):
            mine = jnp.where(is_query & (c // slots == ((r // rows) ^ k)), moved, 0.0).astype(BF)
            fold = ((fc % slots + k * slots) == fs).astype(F32).astype(BF)
            picked = picked + jnp.dot(mine, fold, preferred_element_type=F32)
        grads = lax.dot_general(
            picked.astype(BF), table, (((0,), (0,)), ((), ())), preferred_element_type=F32
        )
        pass_ref[...] = grads[: 2 * slots] * gain_ref[...] * (1.0 / LEN)
        own = head[:rows]
        ec = lax.broadcasted_iota(jnp.int32, (lanes, total), 0)
        er = lax.broadcasted_iota(jnp.int32, (lanes, total), 1)
        spread = ((er // rows == ec // slots) & (er % rows == ec % slots)).astype(F32).astype(BF)
        weights = jnp.dot(own.astype(BF), spread, preferred_element_type=F32).astype(BF)
        result = jnp.dot(weights, table, preferred_element_type=F32)
        question_ref[...] = result[slots + queries :]

    for part in range(own_ref.shape[0] // LEN):
        here = slice(part * LEN, (part + 1) * LEN)
        for k, src in enumerate((own_ref, nb_ref)):
            x = src[here].astype(F32)
            centre = x - jnp.mean(x, axis=-1, keepdims=True)
            inverse = lax.rsqrt(jnp.mean(centre * centre, axis=-1, keepdims=True) + 1e-06)
            slot = k * slots + step * (own_ref.shape[0] // LEN) + part
            scaled = pass_ref[pl.ds(slot, 1), :]
            base = scaled - jnp.mean(scaled, axis=-1, keepdims=True)
            along = jnp.mean(centre * scaled, axis=-1, keepdims=True) * (inverse * inverse)
            bf_ref[k, here] = (inverse * (base - centre * along)).astype(BF)


def resid_grads(slots, queries, own, nb, table, gain):
    tokens, width = own.shape
    total = table.shape[0]
    block = 4 * LEN
    return pl.pallas_call(
        functools.partial(resid_kernel, slots, queries),
        grid=(tokens // block,),
        out_shape=(
            jax.ShapeDtypeStruct((2, tokens, width), BF),
            jax.ShapeDtypeStruct((queries, width), F32),
        ),
        in_specs=[
            pl.BlockSpec((block, width), lambda s: (s, 0)),
            pl.BlockSpec((block, width), lambda s: (s, 0)),
            pl.BlockSpec((total, width), lambda s: (0, 0)),
            pl.BlockSpec((1, width), lambda s: (0, 0)),
        ],
        out_specs=(
            pl.BlockSpec((2, block, width), lambda s: (0, s, 0)),
            pl.BlockSpec((queries, width), lambda s: (0, 0)),
        ),
        scratch_shapes=[pltpu.VMEM((2 * slots, width), F32)],
        compiler_params=params(16),
        cost_estimate=FREE,
        name="resid_grads",
    )(own, nb, table, gain)


def gelu_kernel(half, ids_ref, in_ref, act0, act1, slope0, slope1):
    chip, core, group = ids_ref[0] // 2, ids_ref[0] % 2, ids_ref[1]
    width = act0.shape[1]
    for i in range(width // 128):
        if half:
            rows = 2 * width // half
            a, b = (
                in_ref[:, pl.ds(pl.multiple_of(((chip ^ j) * 2 + core) * rows, 128), 128)].astype(F32)
                for j in (2 * i, 2 * i + 1)
            )
            low = jnp.concatenate([a[:, :64], b[:, :64]], axis=1)
            high = jnp.concatenate([a[:, 64:], b[:, 64:]], axis=1)
        else:
            low = in_ref[:, i * 128 : (i + 1) * 128].astype(F32)
            high = in_ref[:, width + i * 128 : width + (i + 1) * 128].astype(F32)
        pair = jnp.where(group == 0, low, high), jnp.where(group == 0, high, low)
        for z, act, slope in zip(pair, (act0, act1), (slope0, slope1)):
            cdf = 0.5 * (1.0 + lax.erf(z * 0.7071067811865476))
            density = jnp.exp(-0.5 * z * z) * 0.3989422804014327
            act[:, i * 128 : (i + 1) * 128] = (z * cdf).astype(BF)
            slope[:, i * 128 : (i + 1) * 128] = cdf + z * density


def gelu(ids, preact, units, half):
    tokens, width = preact.shape
    block = 256
    out = pl.BlockSpec((block, units // 2), lambda i, ids: (i, 0))
    return pl.pallas_call(
        functools.partial(gelu_kernel, half),
        grid_spec=pltpu.PrefetchScalarGridSpec(
            num_scalar_prefetch=1,
            grid=(tokens // block,),
            in_specs=[pl.BlockSpec((block, width), lambda i, ids: (i, 0))],
            out_specs=[out] * 4,
        ),
        out_shape=[jax.ShapeDtypeStruct((tokens, units // 2), t) for t in (BF, BF, F32, F32)],
        compiler_params=params(8),
        cost_estimate=FREE,
        name="gelu",
    )(ids, preact)


def grad_out_kernel(rows, own_ref, nb_ref, resid_ref, keep_ref, sent_ref):
    contract = (((0,), (0,)), ((), ()))
    out = lax.dot_general(own_ref[...], resid_ref[0], contract, preferred_element_type=F32)
    out = out + lax.dot_general(nb_ref[...], resid_ref[1], contract, preferred_element_type=F32)
    keep_ref[...], sent_ref[...] = halves(out, rows)


def grad_out_part(rows, own, nb, resid):
    tokens, units = own.shape
    width = resid.shape[2]
    block = 256
    return pl.pallas_call(
        functools.partial(grad_out_kernel, rows),
        grid=(units // block,),
        in_specs=[pl.BlockSpec((tokens, block), lambda j: (0, j))] * 2
        + [pl.BlockSpec((2, tokens, width), lambda j: (0, 0, 0))],
        out_specs=[pl.BlockSpec((block // 2, width), lambda j: (j, 0))] * 2,
        out_shape=[jax.ShapeDtypeStruct((units // 2, width), BF)] * 2,
        compiler_params=params(12),
        cost_estimate=FREE,
        name="grad_out",
    )(own, nb, resid)


def grad_in_kernel(
    rows, resid_ref, w_ref, slope_own, slope_nb, own_ref, nb_ref, pre_ref, keep_ref, sent_ref
):
    total = None
    for k, (slope, states) in enumerate(((slope_own, own_ref), (slope_nb, nb_ref))):
        hidden = lax.dot_general(
            resid_ref[k], w_ref[...], (((1,), (1,)), ((), ())), preferred_element_type=F32
        )
        pre = (hidden * slope[...]).astype(BF)
        pre_ref[k] = pre
        out = lax.dot_general(
            pre, states[...], (((0,), (0,)), ((), ())), preferred_element_type=F32
        )
        total = out if total is None else total + out
    keep_ref[...], sent_ref[...] = halves(total, rows)


def grad_in_part(rows, resid, w_out, slope_own, slope_nb, states, states_nb):
    _, tokens, width = resid.shape
    units = w_out.shape[0]
    block = 256
    whole = lambda j: (0, 0)
    return pl.pallas_call(
        functools.partial(grad_in_kernel, rows),
        grid=(units // block,),
        in_specs=[
            pl.BlockSpec((2, tokens, width), lambda j: (0, 0, 0)),
            pl.BlockSpec((block, width), lambda j: (j, 0)),
            pl.BlockSpec((tokens, block), lambda j: (0, j)),
            pl.BlockSpec((tokens, block), lambda j: (0, j)),
            pl.BlockSpec(states.shape, whole),
            pl.BlockSpec(states.shape, whole),
        ],
        out_specs=(
            pl.BlockSpec((2, tokens, block), lambda j: (0, 0, j)),
            pl.BlockSpec((block // 2, width), lambda j: (j, 0)),
            pl.BlockSpec((block // 2, width), lambda j: (j, 0)),
        ),
        out_shape=(
            jax.ShapeDtypeStruct((2, tokens, units), BF),
            jax.ShapeDtypeStruct((units // 2, width), BF),
            jax.ShapeDtypeStruct((units // 2, width), BF),
        ),
        compiler_params=params(18),
        cost_estimate=FREE,
        name="grad_in",
    )(resid, w_out, slope_own, slope_nb, states, states_nb)


def input_nb_kernel(pre0, pre1, w0, w1, out_ref):
    total = jnp.dot(pre0[0], w0[...], preferred_element_type=F32)
    total = total + jnp.dot(pre1[0], w1[...], preferred_element_type=F32)
    out_ref[...] = total.astype(BF)


def input_own_kernel(pre0, pre1, w0, w1, resid_ref, first_ref, second_ref, mark_ref, out_ref):
    total = jnp.dot(pre0[0], w0[...], preferred_element_type=F32)
    total = total + jnp.dot(pre1[0], w1[...], preferred_element_type=F32)
    total = total + resid_ref[0].astype(F32)

    @pl.when(pl.program_id(0) == 0)
    def _():
        out_ref[...] = (total + first_ref[...].astype(F32)).astype(BF)

    @pl.when(pl.program_id(0) == 1)
    def _():
        out_ref[...] = (total + second_ref[...].astype(F32)).astype(BF)


def input_nb(pre, w_in, part):
    _, tokens, units = pre[0].shape
    width = w_in[0].shape[1]
    block = tokens // 2
    return pl.pallas_call(
        input_nb_kernel,
        grid=(1,),
        in_specs=[pl.BlockSpec((1, block, units), lambda i: (1, part, 0))] * 2
        + [pl.BlockSpec((units, width), lambda i: (0, 0))] * 2,
        out_specs=pl.BlockSpec((block, width), lambda i: (0, 0)),
        out_shape=jax.ShapeDtypeStruct((block, width), BF),
        compiler_params=params(12),
        cost_estimate=FREE,
        name="input_nb",
    )(*pre, *w_in)


def input_own(pre, w_in, resid, first, second, mark):
    _, tokens, units = pre[0].shape
    width = w_in[0].shape[1]
    block = tokens // 2
    whole = lambda i: (0, 0)
    return pl.pallas_call(
        input_own_kernel,
        grid=(2,),
        in_specs=[pl.BlockSpec((1, block, units), lambda i: (0, i, 0))] * 2
        + [pl.BlockSpec((units, width), whole)] * 2
        + [pl.BlockSpec((1, block, width), lambda i: (0, i, 0))]
        + [pl.BlockSpec((block, width), whole)] * 2
        + [pl.BlockSpec(memory_space=pl.ANY)],
        out_specs=pl.BlockSpec((block, width), lambda i: (i, 0)),
        out_shape=jax.ShapeDtypeStruct((tokens, width), BF),
        compiler_params=params(16),
        cost_estimate=FREE,
        name="input_own",
    )(*pre, *w_in, resid, first, second, mark)


def tick_kernel(in_ref, out_ref):
    out_ref[...] = in_ref[...]


def tick(x, count):
    vmem = pl.BlockSpec(memory_space=pltpu.VMEM)
    return pl.pallas_call(
        tick_kernel,
        in_specs=[vmem],
        out_specs=vmem,
        out_shape=jax.ShapeDtypeStruct(x.shape, x.dtype),
        compiler_params=params(1),
        cost_estimate=pl.CostEstimate(flops=count * TICK, bytes_accessed=0, transcendentals=0),
        name="tick",
    )(x)


class Order:
    def __init__(self, mark):
        self.mark = mark

    def gate(self, *args):
        *args, self.mark = lax.optimization_barrier((*args, self.mark))
        return args

    def __call__(self, work, *args, ticks=1):
        out = work(*self.gate(*args))
        leaves, tree = jax.tree.flatten(out)
        out = jax.tree.unflatten(tree, self.gate(*leaves))
        if ticks:
            self.mark = tick(self.mark, ticks)
        return out


def place(mask, masks):
    return sum(1 for other in masks if other > mask)


def run(kernel, name, shapes, *args):
    vmem = pl.BlockSpec(memory_space=pltpu.VMEM)
    return pl.pallas_call(
        kernel,
        in_specs=[vmem] * len(args),
        out_specs=[vmem] * len(shapes),
        out_shape=[jax.ShapeDtypeStruct(s, BF) for s in shapes],
        compiler_params=params(6),
        cost_estimate=FREE,
        name=name,
    )(*args)


def join_kernel(rows, a_ref, b_ref, out_ref):
    total, width = a_ref.shape
    if rows % 16:
        a, b = (x[...].astype(F32).reshape(total // rows, rows, width) for x in (a_ref, b_ref))
        out_ref[...] = jnp.stack([a, b], axis=1).reshape(2 * total, width).astype(BF)
        return
    for i in range(total // rows):
        part = slice(i * rows, (i + 1) * rows)
        out_ref[2 * i * rows : (2 * i + 1) * rows] = a_ref[part]
        out_ref[(2 * i + 1) * rows : (2 * i + 2) * rows] = b_ref[part]


def join(a, b, rows):
    total, width = a.shape
    return run(functools.partial(join_kernel, rows), "join", [(2 * total, width)], a, b)[0]


def halves(x, rows):
    total, width = x.shape
    x = x.reshape(total // (2 * rows), 2, rows, width)
    return [x[:, k].reshape(total // 2, width).astype(BF) for k in range(2)]


def fold_kernel(rows, a_ref, b_ref, keep_ref, sent_ref):
    total = a_ref[...].astype(F32) + b_ref[...].astype(F32)
    keep_ref[...], sent_ref[...] = halves(total, rows)


def fold(a, b, rows):
    total, width = a.shape
    return run(functools.partial(fold_kernel, rows), "fold", [(total // 2, width)] * 2, a, b)


def total_kernel(ids_ref, *refs):
    *parts, mark_ref, out_ref = refs
    rows = out_ref.shape[0] // 2
    sums = [a[...].astype(F32) + b[...].astype(F32) for a, b in zip(parts[::2], parts[1::2])]
    if len(sums) == 1:
        sums = [sums[0][:rows], sums[0][rows:]]
    for k, x in enumerate(sums):
        start = k * rows + (1 - 2 * k) * ids_ref[1] * rows
        out_ref[pl.ds(pl.multiple_of(start, rows), rows)] = x


def total(ids, mark, *chains):
    parts = [x for chain in chains for x in (chain.keep, chain.came)]
    rows = sum(chain.keep.shape[0] for chain in chains)
    vmem = pl.BlockSpec(memory_space=pltpu.VMEM)
    return pl.pallas_call(
        total_kernel,
        in_specs=[pl.BlockSpec(memory_space=pltpu.SMEM)] + [vmem] * (len(parts) + 1),
        out_shape=jax.ShapeDtypeStruct((rows, parts[0].shape[1]), F32),
        compiler_params=params(6),
        cost_estimate=FREE,
        name="total",
    )(ids, *parts, mark)


class Chain:
    def __init__(self, order, masks, rows):
        self.order, self.left, self.done, self.rows = order, list(masks), [], rows
        self.steps = 3

    def due(self, last):
        self.steps -= 1
        while len(self.left) > max(self.steps, last):
            yield self.left[0]


class Gather(Chain):
    def __init__(self, order, x, masks):
        super().__init__(order, masks, x.shape[0])
        self.x = x
        self.steps = min(len(self.left), 4 if masks[-1] == 1 else 3)

    def send(self):
        self.came = swap(*self.order.gate(self.x), self.left[0])

    def step(self, ticks):
        first = True
        for mask in self.due(0):
            if not first:
                self.send()
            first = False
            rows = self.rows << (len(self.done) - place(mask, self.done))
            self.before, self.arrived, self.block = self.x, self.came, rows
            self.x = self.order(lambda a, b: join(a, b, rows), self.x, self.came, ticks=ticks)
            self.done.append(self.left.pop(0))


class Scatter(Chain):
    def block(self):
        return self.rows << (len(self.left) - 1 - place(self.left[0], self.left))

    def start(self, make, *args):
        rows = self.block()
        *extra, self.keep, self.sent = self.order(lambda *x: make(rows, *x), *args, ticks=0)
        return extra

    def send(self):
        self.came = swap(*self.order.gate(self.sent), self.left[0])

    def step(self, ticks):
        first = True
        for _ in self.due(1):
            if not first:
                self.send()
            first = False
            self.left.pop(0)
            rows = self.block()
            self.keep, self.sent = self.order(
                lambda a, b: fold(a, b, rows), self.keep, self.came, ticks=ticks
            )


def shards(
    passage_states,
    saved_preact,
    saved_resid,
    w_in,
    w_out,
    norm_gain,
    query_emb,
    score_grads,
    retrieved,
    placement_map,
    live_counts,
):
    n = lax.axis_size("psg")
    shared = lax.axis_size("groups") == 2
    me = lax.axis_index("psg").astype(jnp.int32)
    group = lax.axis_index("groups").astype(jnp.int32) if shared else jnp.int32(0)
    ids = jnp.stack([me, group])
    core, chip = me % 2, me // 2
    half = n // 2
    tokens, width = saved_resid.shape
    rows = w_in.shape[0]
    units = half * rows
    slots = tokens // LEN
    queries = query_emb.shape[0]
    masks = [1 << b for b in range(1, n.bit_length() - 1)]
    orders = {
        "up": masks,
        "down": masks[::-1],
        "side": masks[1::-1] + masks[2:],
        "far": masks[:1] + masks[:0:-1],
        "mixed": masks[1:2] + masks[:1:-1] + masks[:1],
        "low": masks[:1:-1] + masks[:2],
    }
    gain = norm_gain.reshape(1, width)
    whole_tiles = rows == 128
    order = Order(jnp.zeros((8, 128), F32) + me.astype(F32))

    def cross(x):
        return lax.ppermute(x, "groups", [(0, 1), (1, 0)])

    preact_own = columns = saved_preact
    if not whole_tiles:
        view = saved_preact.reshape(tokens, half, 2, 2, rows // 2)
        view = jnp.take(view, jnp.arange(half) ^ chip, axis=1).transpose(2, 0, 3, 1, 4)
        view = view.reshape(2, tokens, units)
        preact_own = lax.dynamic_index_in_dim(view, core, axis=0, keepdims=False)
        columns = lax.dynamic_index_in_dim(view, 1 - core, axis=0, keepdims=False)
    mine_out, mine_in = (
        lax.dynamic_slice_in_dim(w, group * (rows // 2), rows // 2, 0) for w in (w_out, w_in)
    )
    v, swapped = {}, {"pre": columns, "resid": saved_resid, "states": passage_states}
    chains = {
        "out": Gather(order, mine_out, orders[ORDERS["out"]]),
        "inp": Gather(order, mine_in, orders[ORDERS["inp"]]),
    }
    for name in ("go0", "go1", "gi0", "gi1"):
        chains[name] = Scatter(order, orders[ORDERS[name]], rows // 2)

    def weight(chain, first, second):
        return order(lambda a, b: join(a, b, chain.block), v.pop(first), v.pop(second), ticks=0)

    for word in SCHEDULE:
        name, _, ticks = word.partition(":")
        ticks = int(ticks or 0)
        chain = chains.get(name.rstrip(">"))
        if name[:-1] in swapped and name.endswith(">"):
            x = swapped[name[:-1]]
            v[name[:-1]] = swap(*order.gate(x), 1) if ticks else swap(x, 1)
        elif name.endswith(">"):
            chain.send()
        elif name.endswith("?"):
            if name[:-1] in chains:
                chain = chains[name[:-1]]
                chain.came, = order.gate(chain.came)
            for key in [k for k in v if k.startswith(name[:-1])]:
                v[key], = order.gate(v[key])
            if ticks:
                order.mark = tick(order.mark, ticks)
        elif name in ("out", "inp", "small"):
            chain.step(ticks)
        elif name == "pack":
            table = order(
                lambda *args: pack(slots, ids, *args),
                placement_map, live_counts, saved_resid, gain, query_emb, score_grads, retrieved, ticks=0,
            )
            chains["small"] = Gather(order, table, orders["far"] + [1])
        elif name in ("gelu0", "gelu1"):
            x = preact_own if name == "gelu0" else v["pre"]
            v[name] = order(lambda x: gelu(ids, x, units, half if whole_tiles else 0), x, ticks=0)
        elif name == "resid":
            resid_bf, question_grad = order(
                lambda a, b, c: resid_grads(slots, queries, a, b, c, gain),
                saved_resid, v["resid"], chains["small"].x, ticks=0,
            )
        elif name in ("go0", "go1", "gi0", "gi1"):
            k = int(name[2])
            if chain.steps < 3 or hasattr(chain, "keep"):
                chain.step(ticks)
            elif name[:2] == "go":
                chain.start(grad_out_part, v["gelu0"][k], v["gelu1"][k], resid_bf)
            else:
                v["p%d" % k], = chain.start(
                    grad_in_part, resid_bf, chains["out"].x if k == 0 else out1,
                    v["gelu0"][2 + k], v["gelu1"][2 + k], passage_states, v["states"],
                )
        elif name == "xa":
            v["xa"] = cross(*order.gate(chains["out"].x))
        elif name == "xb":
            v["xb"] = cross(*order.gate(chains["out"].arrived))
        elif name == "ia":
            v["ia"] = cross(*order.gate(chains["inp"].before if chains["inp"].steps == 0 else chains["inp"].x))
        elif name == "ib":
            v["ib"] = cross(*order.gate(chains["inp"].arrived))
        elif name == "wout":
            out1 = weight(chains["out"], "xa", "xb")
        elif name == "win":
            w_in = (chains["inp"].x, weight(chains["inp"], "ia", "ib"))
        elif name in ("nb0", "nb1"):
            k = int(name[2])
            v[name] = swap(order(lambda *w: input_nb((v["p0"], v["p1"]), w, k), *w_in, ticks=0), 1)
        elif name == "own":
            mark = order.mark
            input_grad = order(
                lambda a, b: input_own((v["p0"], v["p1"]), w_in, resid_bf, a, b, mark), v["nb0"], v["nb1"],
                ticks=0,
            )
        elif name in ("tgo", "tgi"):
            pair = [chains[name[1:] + k] for k in "01"]
            pair[0].came, pair[1].came = order.gate(pair[0].came, pair[1].came)
            mark = order.mark
            v[name] = order(lambda *x: total(ids, mark, *pair), pair[0].came, ticks=0)
        else:
            raise ValueError(word)
    return (input_grad, v["tgi"], v["tgo"], question_grad)


def solution(mesh):
    both = P(("groups", "psg"), None)
    return jax.shard_map(
        shards,
        mesh=mesh,
        in_specs=(both, both, both, P("psg", None), P("psg", None), P(), both, both, both, P("groups"), P("groups")),
        out_specs=(both, both, both, both),
        check_vma=False,
    )
```

```python
import functools

import jax
import jax.numpy as jnp
from jax import lax
from jax.experimental import pallas as pl
from jax.experimental.pallas import tpu as pltpu
from jax.sharding import PartitionSpec as P

LEN = 128
TICK = 100_000_000
SCHEDULE = (
    "inp>", "pre>", "resid>", "states>", "out>", "pack", "out:30", "out>", "resid?", "small>",
    "gelu0", "small:1", "small>", "inp:1", "out:1", "out>", "xa", "small:30", "small>", "inp>",
    "gelu1", "small:30", "states?", "small>", "small:1", "ia?", "resid", "out:1", "xb", "xa?",
    "inp:1", "xa?", "inp>", "go1", "ia?", "gi0", "go0", "go0>", "go1>", "gi0>", "inp:1", "wout",
    "gi1:30", "gi1>", "ia", "go0:1", "go0>", "gi0:1", "ia?", "gi0>", "ib", "go1:1", "go1>", "gi1:1",
    "gi1>", "go0:1", "go0>", "gi0:10", "gi0>", "win", "nb0", "go1:1", "go1>", "nb1", "go0?", "tgo",
    "gi1:30", "gi1>", "own", "nb?", "tgi",
)
ORDERS = {"out": "down", "inp": "far", "go0": "side", "go1": "up", "gi0": "far", "gi1": "side"}
BF = jnp.bfloat16
F32 = jnp.float32
PACK_MIB = 63


def params(mib):
    return pltpu.CompilerParams(vmem_limit_bytes=mib << 20)


FREE = pl.CostEstimate(flops=0, bytes_accessed=0, transcendentals=0)


def swap(x, mask):
    n = lax.axis_size("psg")
    return lax.ppermute(x, "psg", [(i, i ^ mask) for i in range(n)])


def pack_kernel(
    slots, ids_ref, place_in, live_in, resid_in, gain_in, query_in, score_in, ret_in, out_ref,
    place_ref, live_ref, resid_ref, gain_ref, query_ref, score_ref, ret_ref, sems,
):
    me = ids_ref[0]
    passages = place_ref.shape[0]
    width = out_ref.shape[1]
    queries, picks = ret_ref.shape
    inputs = (resid_in, place_in, live_in, ret_in, score_in, query_in, gain_in)
    targets = (resid_ref, place_ref, live_ref, ret_ref, score_ref, query_ref, gain_ref)
    small = [pltpu.make_async_copy(a, b, sems.at[i]) for i, (a, b) in enumerate(zip(inputs, targets))]
    for copy in small:
        copy.start()
    for copy in small[1:]:
        copy.wait()
    ids = ret_ref[...]

    def look(i, placed):
        p = place_ref[i]
        owner = p // slots
        slot = p % slots
        rel = (owner ^ me) * slots + slot
        rel = jnp.where(slot < live_ref[owner], rel, -1)
        return jnp.where(ids == i, rel, placed)

    placed = lax.fori_loop(0, passages, look, jnp.full(ids.shape, -1, jnp.int32), unroll=8)
    score = score_ref[...].astype(F32)
    lanes = max(passages, 128)
    cols = lax.broadcasted_iota(jnp.int32, (queries, lanes), 1)
    pairs = jnp.zeros((queries, lanes), F32)
    for k in range(picks):
        pairs = pairs + jnp.where(cols == placed[:, k : k + 1], score[:, k : k + 1], 0.0)
    if lanes < width:
        pairs = jnp.concatenate([pairs, jnp.zeros((queries, width - lanes), F32)], axis=1)
    small[0].wait()
    rows = []
    for s in range(slots):
        x = resid_ref[s * LEN : (s + 1) * LEN, :].astype(F32)
        centre = x - jnp.mean(x, axis=-1, keepdims=True)
        inverse = lax.rsqrt(jnp.mean(centre * centre, axis=-1, keepdims=True) + 1e-06)
        rows.append(jnp.mean(centre * inverse, axis=0, keepdims=True) * gain_ref[...])
    out_ref[...] = jnp.concatenate(rows + [query_ref[...].astype(F32), pairs], axis=0).astype(BF)


def pack(slots, ids, placement, live, resid, gain, query, score, retrieved):
    width = resid.shape[1]
    queries = query.shape[0]
    smem = pl.BlockSpec(memory_space=pltpu.SMEM)
    hbm = pl.BlockSpec(memory_space=pltpu.HBM)
    scratch = [pltpu.SMEM(x.shape, x.dtype) for x in (placement, live)]
    scratch += [pltpu.VMEM(x.shape, x.dtype) for x in (resid, gain, query, score, retrieved)]
    return pl.pallas_call(
        functools.partial(pack_kernel, slots),
        out_shape=jax.ShapeDtypeStruct((slots + 2 * queries, width), BF),
        in_specs=[smem] + [hbm] * 7,
        out_specs=pl.BlockSpec(memory_space=pltpu.VMEM),
        scratch_shapes=scratch + [pltpu.SemaphoreType.DMA((7,))],
        compiler_params=params(PACK_MIB),
        cost_estimate=FREE,
        name="pack",
    )(ids, placement, live, resid, gain, query, score, retrieved)


def resid_kernel(slots, queries, own_ref, nb_ref, all_ref, gain_ref, bf_ref, question_ref, pass_ref):
    step = pl.program_id(0)
    rows = slots + 2 * queries
    total = all_ref.shape[0]
    lanes = max(total // rows * slots, 128)

    @pl.when(step == 0)
    def _():
        table = all_ref[...]
        head = all_ref[:, :lanes].astype(F32)
        r = lax.broadcasted_iota(jnp.int32, (total, lanes), 0)
        c = lax.broadcasted_iota(jnp.int32, (total, lanes), 1)
        inside = r % rows
        moved = pltpu.roll(head, total - queries, 0)
        is_query = (inside >= slots) & (inside < slots + queries)
        fc = lax.broadcasted_iota(jnp.int32, (lanes, 128), 0)
        fs = lax.broadcasted_iota(jnp.int32, (lanes, 128), 1)
        picked = jnp.zeros((total, 128), F32)
        for k in range(2):
            mine = jnp.where(is_query & (c // slots == ((r // rows) ^ k)), moved, 0.0).astype(BF)
            fold = ((fc % slots + k * slots) == fs).astype(F32).astype(BF)
            picked = picked + jnp.dot(mine, fold, preferred_element_type=F32)
        grads = lax.dot_general(
            picked.astype(BF), table, (((0,), (0,)), ((), ())), preferred_element_type=F32
        )
        pass_ref[...] = grads[: 2 * slots] * gain_ref[...] * (1.0 / LEN)
        own = head[:rows]
        ec = lax.broadcasted_iota(jnp.int32, (lanes, total), 0)
        er = lax.broadcasted_iota(jnp.int32, (lanes, total), 1)
        spread = ((er // rows == ec // slots) & (er % rows == ec % slots)).astype(F32).astype(BF)
        weights = jnp.dot(own.astype(BF), spread, preferred_element_type=F32).astype(BF)
        result = jnp.dot(weights, table, preferred_element_type=F32)
        question_ref[...] = result[slots + queries :]

    for part in range(own_ref.shape[0] // LEN):
        here = slice(part * LEN, (part + 1) * LEN)
        for k, src in enumerate((own_ref, nb_ref)):
            x = src[here].astype(F32)
            centre = x - jnp.mean(x, axis=-1, keepdims=True)
            inverse = lax.rsqrt(jnp.mean(centre * centre, axis=-1, keepdims=True) + 1e-06)
            slot = k * slots + step * (own_ref.shape[0] // LEN) + part
            scaled = pass_ref[pl.ds(slot, 1), :]
            base = scaled - jnp.mean(scaled, axis=-1, keepdims=True)
            along = jnp.mean(centre * scaled, axis=-1, keepdims=True) * (inverse * inverse)
            bf_ref[k, here] = (inverse * (base - centre * along)).astype(BF)


def resid_grads(slots, queries, own, nb, table, gain):
    tokens, width = own.shape
    total = table.shape[0]
    block = 4 * LEN
    return pl.pallas_call(
        functools.partial(resid_kernel, slots, queries),
        grid=(tokens // block,),
        out_shape=(
            jax.ShapeDtypeStruct((2, tokens, width), BF),
            jax.ShapeDtypeStruct((queries, width), F32),
        ),
        in_specs=[
            pl.BlockSpec((block, width), lambda s: (s, 0)),
            pl.BlockSpec((block, width), lambda s: (s, 0)),
            pl.BlockSpec((total, width), lambda s: (0, 0)),
            pl.BlockSpec((1, width), lambda s: (0, 0)),
        ],
        out_specs=(
            pl.BlockSpec((2, block, width), lambda s: (0, s, 0)),
            pl.BlockSpec((queries, width), lambda s: (0, 0)),
        ),
        scratch_shapes=[pltpu.VMEM((2 * slots, width), F32)],
        compiler_params=params(16),
        cost_estimate=FREE,
        name="resid_grads",
    )(own, nb, table, gain)


def gelu_kernel(half, ids_ref, in_ref, act0, act1, slope0, slope1):
    chip, core, group = ids_ref[0] // 2, ids_ref[0] % 2, ids_ref[1]
    width = act0.shape[1]
    for i in range(width // 128):
        if half:
            rows = 2 * width // half
            a, b = (
                in_ref[:, pl.ds(pl.multiple_of(((chip ^ j) * 2 + core) * rows, 128), 128)].astype(F32)
                for j in (2 * i, 2 * i + 1)
            )
            low = jnp.concatenate([a[:, :64], b[:, :64]], axis=1)
            high = jnp.concatenate([a[:, 64:], b[:, 64:]], axis=1)
        else:
            low = in_ref[:, i * 128 : (i + 1) * 128].astype(F32)
            high = in_ref[:, width + i * 128 : width + (i + 1) * 128].astype(F32)
        pair = jnp.where(group == 0, low, high), jnp.where(group == 0, high, low)
        for z, act, slope in zip(pair, (act0, act1), (slope0, slope1)):
            cdf = 0.5 * (1.0 + lax.erf(z * 0.7071067811865476))
            density = jnp.exp(-0.5 * z * z) * 0.3989422804014327
            act[:, i * 128 : (i + 1) * 128] = (z * cdf).astype(BF)
            slope[:, i * 128 : (i + 1) * 128] = cdf + z * density


def gelu(ids, preact, units, half):
    tokens, width = preact.shape
    block = 256
    out = pl.BlockSpec((block, units // 2), lambda i, ids: (i, 0))
    return pl.pallas_call(
        functools.partial(gelu_kernel, half),
        grid_spec=pltpu.PrefetchScalarGridSpec(
            num_scalar_prefetch=1,
            grid=(tokens // block,),
            in_specs=[pl.BlockSpec((block, width), lambda i, ids: (i, 0))],
            out_specs=[out] * 4,
        ),
        out_shape=[jax.ShapeDtypeStruct((tokens, units // 2), t) for t in (BF, BF, F32, F32)],
        compiler_params=params(8),
        cost_estimate=FREE,
        name="gelu",
    )(ids, preact)


def grad_out_kernel(rows, own_ref, nb_ref, resid_ref, keep_ref, sent_ref):
    contract = (((0,), (0,)), ((), ()))
    out = lax.dot_general(own_ref[...], resid_ref[0], contract, preferred_element_type=F32)
    out = out + lax.dot_general(nb_ref[...], resid_ref[1], contract, preferred_element_type=F32)
    keep_ref[...], sent_ref[...] = halves(out, rows)


def grad_out_part(rows, own, nb, resid):
    tokens, units = own.shape
    width = resid.shape[2]
    block = 256
    return pl.pallas_call(
        functools.partial(grad_out_kernel, rows),
        grid=(units // block,),
        in_specs=[pl.BlockSpec((tokens, block), lambda j: (0, j))] * 2
        + [pl.BlockSpec((2, tokens, width), lambda j: (0, 0, 0))],
        out_specs=[pl.BlockSpec((block // 2, width), lambda j: (j, 0))] * 2,
        out_shape=[jax.ShapeDtypeStruct((units // 2, width), BF)] * 2,
        compiler_params=params(12),
        cost_estimate=FREE,
        name="grad_out",
    )(own, nb, resid)


def grad_in_kernel(
    rows, resid_ref, w_ref, slope_own, slope_nb, own_ref, nb_ref, pre_ref, keep_ref, sent_ref
):
    total = None
    for k, (slope, states) in enumerate(((slope_own, own_ref), (slope_nb, nb_ref))):
        hidden = lax.dot_general(
            resid_ref[k], w_ref[...], (((1,), (1,)), ((), ())), preferred_element_type=F32
        )
        pre = (hidden * slope[...]).astype(BF)
        pre_ref[k] = pre
        out = lax.dot_general(
            pre, states[...], (((0,), (0,)), ((), ())), preferred_element_type=F32
        )
        total = out if total is None else total + out
    keep_ref[...], sent_ref[...] = halves(total, rows)


def grad_in_part(rows, resid, w_out, slope_own, slope_nb, states, states_nb):
    _, tokens, width = resid.shape
    units = w_out.shape[0]
    block = 256
    whole = lambda j: (0, 0)
    return pl.pallas_call(
        functools.partial(grad_in_kernel, rows),
        grid=(units // block,),
        in_specs=[
            pl.BlockSpec((2, tokens, width), lambda j: (0, 0, 0)),
            pl.BlockSpec((block, width), lambda j: (j, 0)),
            pl.BlockSpec((tokens, block), lambda j: (0, j)),
            pl.BlockSpec((tokens, block), lambda j: (0, j)),
            pl.BlockSpec(states.shape, whole),
            pl.BlockSpec(states.shape, whole),
        ],
        out_specs=(
            pl.BlockSpec((2, tokens, block), lambda j: (0, 0, j)),
            pl.BlockSpec((block // 2, width), lambda j: (j, 0)),
            pl.BlockSpec((block // 2, width), lambda j: (j, 0)),
        ),
        out_shape=(
            jax.ShapeDtypeStruct((2, tokens, units), BF),
            jax.ShapeDtypeStruct((units // 2, width), BF),
            jax.ShapeDtypeStruct((units // 2, width), BF),
        ),
        compiler_params=params(18),
        cost_estimate=FREE,
        name="grad_in",
    )(resid, w_out, slope_own, slope_nb, states, states_nb)


def input_nb_kernel(pre0, pre1, w0, w1, out_ref):
    total = jnp.dot(pre0[0], w0[...], preferred_element_type=F32)
    total = total + jnp.dot(pre1[0], w1[...], preferred_element_type=F32)
    out_ref[...] = total.astype(BF)


def input_own_kernel(pre0, pre1, w0, w1, resid_ref, first_ref, second_ref, mark_ref, out_ref):
    total = jnp.dot(pre0[0], w0[...], preferred_element_type=F32)
    total = total + jnp.dot(pre1[0], w1[...], preferred_element_type=F32)
    total = total + resid_ref[0].astype(F32)

    @pl.when(pl.program_id(0) == 0)
    def _():
        out_ref[...] = (total + first_ref[...].astype(F32)).astype(BF)

    @pl.when(pl.program_id(0) == 1)
    def _():
        out_ref[...] = (total + second_ref[...].astype(F32)).astype(BF)


def input_nb(pre, w_in, part):
    _, tokens, units = pre[0].shape
    width = w_in[0].shape[1]
    block = tokens // 2
    return pl.pallas_call(
        input_nb_kernel,
        grid=(1,),
        in_specs=[pl.BlockSpec((1, block, units), lambda i: (1, part, 0))] * 2
        + [pl.BlockSpec((units, width), lambda i: (0, 0))] * 2,
        out_specs=pl.BlockSpec((block, width), lambda i: (0, 0)),
        out_shape=jax.ShapeDtypeStruct((block, width), BF),
        compiler_params=params(12),
        cost_estimate=FREE,
        name="input_nb",
    )(*pre, *w_in)


def input_own(pre, w_in, resid, first, second, mark):
    _, tokens, units = pre[0].shape
    width = w_in[0].shape[1]
    block = tokens // 2
    whole = lambda i: (0, 0)
    return pl.pallas_call(
        input_own_kernel,
        grid=(2,),
        in_specs=[pl.BlockSpec((1, block, units), lambda i: (0, i, 0))] * 2
        + [pl.BlockSpec((units, width), whole)] * 2
        + [pl.BlockSpec((1, block, width), lambda i: (0, i, 0))]
        + [pl.BlockSpec((block, width), whole)] * 2
        + [pl.BlockSpec(memory_space=pl.ANY)],
        out_specs=pl.BlockSpec((block, width), lambda i: (i, 0)),
        out_shape=jax.ShapeDtypeStruct((tokens, width), BF),
        compiler_params=params(16),
        cost_estimate=FREE,
        name="input_own",
    )(*pre, *w_in, resid, first, second, mark)


def tick_kernel(in_ref, out_ref):
    out_ref[...] = in_ref[...]


def tick(x, count):
    vmem = pl.BlockSpec(memory_space=pltpu.VMEM)
    return pl.pallas_call(
        tick_kernel,
        in_specs=[vmem],
        out_specs=vmem,
        out_shape=jax.ShapeDtypeStruct(x.shape, x.dtype),
        compiler_params=params(1),
        cost_estimate=pl.CostEstimate(flops=count * TICK, bytes_accessed=0, transcendentals=0),
        name="tick",
    )(x)


class Order:
    def __init__(self, mark):
        self.mark = mark

    def gate(self, *args):
        *args, self.mark = lax.optimization_barrier((*args, self.mark))
        return args

    def __call__(self, work, *args, ticks=1):
        out = work(*self.gate(*args))
        leaves, tree = jax.tree.flatten(out)
        out = jax.tree.unflatten(tree, self.gate(*leaves))
        if ticks:
            self.mark = tick(self.mark, ticks)
        return out


def place(mask, masks):
    return sum(1 for other in masks if other > mask)


def run(kernel, name, shapes, *args):
    vmem = pl.BlockSpec(memory_space=pltpu.VMEM)
    return pl.pallas_call(
        kernel,
        in_specs=[vmem] * len(args),
        out_specs=[vmem] * len(shapes),
        out_shape=[jax.ShapeDtypeStruct(s, BF) for s in shapes],
        compiler_params=params(6),
        cost_estimate=FREE,
        name=name,
    )(*args)


def join_kernel(rows, a_ref, b_ref, out_ref):
    total, width = a_ref.shape
    if rows % 16:
        a, b = (x[...].astype(F32).reshape(total // rows, rows, width) for x in (a_ref, b_ref))
        out_ref[...] = jnp.stack([a, b], axis=1).reshape(2 * total, width).astype(BF)
        return
    for i in range(total // rows):
        part = slice(i * rows, (i + 1) * rows)
        out_ref[2 * i * rows : (2 * i + 1) * rows] = a_ref[part]
        out_ref[(2 * i + 1) * rows : (2 * i + 2) * rows] = b_ref[part]


def join(a, b, rows):
    total, width = a.shape
    return run(functools.partial(join_kernel, rows), "join", [(2 * total, width)], a, b)[0]


def halves(x, rows):
    total, width = x.shape
    x = x.reshape(total // (2 * rows), 2, rows, width)
    return [x[:, k].reshape(total // 2, width).astype(BF) for k in range(2)]


def fold_kernel(rows, a_ref, b_ref, keep_ref, sent_ref):
    total = a_ref[...].astype(F32) + b_ref[...].astype(F32)
    keep_ref[...], sent_ref[...] = halves(total, rows)


def fold(a, b, rows):
    total, width = a.shape
    return run(functools.partial(fold_kernel, rows), "fold", [(total // 2, width)] * 2, a, b)


def total_kernel(ids_ref, *refs):
    *parts, mark_ref, out_ref = refs
    rows = out_ref.shape[0] // 2
    sums = [a[...].astype(F32) + b[...].astype(F32) for a, b in zip(parts[::2], parts[1::2])]
    if len(sums) == 1:
        sums = [sums[0][:rows], sums[0][rows:]]
    for k, x in enumerate(sums):
        start = k * rows + (1 - 2 * k) * ids_ref[1] * rows
        out_ref[pl.ds(pl.multiple_of(start, rows), rows)] = x


def total(ids, mark, *chains):
    parts = [x for chain in chains for x in (chain.keep, chain.came)]
    rows = sum(chain.keep.shape[0] for chain in chains)
    vmem = pl.BlockSpec(memory_space=pltpu.VMEM)
    return pl.pallas_call(
        total_kernel,
        in_specs=[pl.BlockSpec(memory_space=pltpu.SMEM)] + [vmem] * (len(parts) + 1),
        out_shape=jax.ShapeDtypeStruct((rows, parts[0].shape[1]), F32),
        compiler_params=params(6),
        cost_estimate=FREE,
        name="total",
    )(ids, *parts, mark)


class Chain:
    def __init__(self, order, masks, rows):
        self.order, self.left, self.done, self.rows = order, list(masks), [], rows
        self.steps = 3

    def due(self, last):
        self.steps -= 1
        while len(self.left) > max(self.steps, last):
            yield self.left[0]


class Gather(Chain):
    def __init__(self, order, x, masks):
        super().__init__(order, masks, x.shape[0])
        self.x = x
        self.steps = min(len(self.left), 4 if masks[-1] == 1 else 3)

    def send(self):
        self.came = swap(*self.order.gate(self.x), self.left[0])

    def step(self, ticks):
        first = True
        for mask in self.due(0):
            if not first:
                self.send()
            first = False
            rows = self.rows << (len(self.done) - place(mask, self.done))
            self.before, self.arrived, self.block = self.x, self.came, rows
            self.x = self.order(lambda a, b: join(a, b, rows), self.x, self.came, ticks=ticks)
            self.done.append(self.left.pop(0))


class Scatter(Chain):
    def block(self):
        return self.rows << (len(self.left) - 1 - place(self.left[0], self.left))

    def start(self, make, *args):
        rows = self.block()
        *extra, self.keep, self.sent = self.order(lambda *x: make(rows, *x), *args, ticks=0)
        return extra

    def send(self):
        self.came = swap(*self.order.gate(self.sent), self.left[0])

    def step(self, ticks):
        first = True
        for _ in self.due(1):
            if not first:
                self.send()
            first = False
            self.left.pop(0)
            rows = self.block()
            self.keep, self.sent = self.order(
                lambda a, b: fold(a, b, rows), self.keep, self.came, ticks=ticks
            )


def shards(
    passage_states,
    saved_preact,
    saved_resid,
    w_in,
    w_out,
    norm_gain,
    query_emb,
    score_grads,
    retrieved,
    placement_map,
    live_counts,
):
    n = lax.axis_size("psg")
    shared = lax.axis_size("groups") == 2
    me = lax.axis_index("psg").astype(jnp.int32)
    group = lax.axis_index("groups").astype(jnp.int32) if shared else jnp.int32(0)
    ids = jnp.stack([me, group])
    core, chip = me % 2, me // 2
    half = n // 2
    tokens, width = saved_resid.shape
    rows = w_in.shape[0]
    units = half * rows
    slots = tokens // LEN
    queries = query_emb.shape[0]
    masks = [1 << b for b in range(1, n.bit_length() - 1)]
    orders = {
        "up": masks,
        "down": masks[::-1],
        "side": masks[1::-1] + masks[2:],
        "far": masks[:1] + masks[:0:-1],
        "mixed": masks[1:2] + masks[:1:-1] + masks[:1],
        "low": masks[:1:-1] + masks[:2],
    }
    gain = norm_gain.reshape(1, width)
    whole_tiles = rows == 128
    order = Order(jnp.zeros((8, 128), F32) + me.astype(F32))

    def cross(x):
        return lax.ppermute(x, "groups", [(0, 1), (1, 0)])

    preact_own = columns = saved_preact
    if not whole_tiles:
        view = saved_preact.reshape(tokens, half, 2, 2, rows // 2)
        view = jnp.take(view, jnp.arange(half) ^ chip, axis=1).transpose(2, 0, 3, 1, 4)
        view = view.reshape(2, tokens, units)
        preact_own = lax.dynamic_index_in_dim(view, core, axis=0, keepdims=False)
        columns = lax.dynamic_index_in_dim(view, 1 - core, axis=0, keepdims=False)
    mine_out, mine_in = (
        lax.dynamic_slice_in_dim(w, group * (rows // 2), rows // 2, 0) for w in (w_out, w_in)
    )
    v, swapped = {}, {"pre": columns, "resid": saved_resid, "states": passage_states}
    chains = {
        "out": Gather(order, mine_out, orders[ORDERS["out"]]),
        "inp": Gather(order, mine_in, orders[ORDERS["inp"]]),
    }
    for name in ("go0", "go1", "gi0", "gi1"):
        chains[name] = Scatter(order, orders[ORDERS[name]], rows // 2)

    def weight(chain, first, second):
        return order(lambda a, b: join(a, b, chain.block), v.pop(first), v.pop(second), ticks=0)

    for word in SCHEDULE:
        name, _, ticks = word.partition(":")
        ticks = int(ticks or 0)
        chain = chains.get(name.rstrip(">"))
        if name[:-1] in swapped and name.endswith(">"):
            x = swapped[name[:-1]]
            v[name[:-1]] = swap(*order.gate(x), 1) if ticks else swap(x, 1)
        elif name.endswith(">"):
            chain.send()
        elif name.endswith("?"):
            if name[:-1] in chains:
                chain = chains[name[:-1]]
                chain.came, = order.gate(chain.came)
            for key in [k for k in v if k.startswith(name[:-1])]:
                v[key], = order.gate(v[key])
            if ticks:
                order.mark = tick(order.mark, ticks)
        elif name in ("out", "inp", "small"):
            chain.step(ticks)
        elif name == "pack":
            table = order(
                lambda *args: pack(slots, ids, *args),
                placement_map, live_counts, saved_resid, gain, query_emb, score_grads, retrieved, ticks=0,
            )
            chains["small"] = Gather(order, table, orders["far"] + [1])
        elif name in ("gelu0", "gelu1"):
            x = preact_own if name == "gelu0" else v["pre"]
            v[name] = order(lambda x: gelu(ids, x, units, half if whole_tiles else 0), x, ticks=0)
        elif name == "resid":
            resid_bf, question_grad = order(
                lambda a, b, c: resid_grads(slots, queries, a, b, c, gain),
                saved_resid, v["resid"], chains["small"].x, ticks=0,
            )
        elif name in ("go0", "go1", "gi0", "gi1"):
            k = int(name[2])
            if chain.steps < 3 or hasattr(chain, "keep"):
                chain.step(ticks)
            elif name[:2] == "go":
                chain.start(grad_out_part, v["gelu0"][k], v["gelu1"][k], resid_bf)
            else:
                v["p%d" % k], = chain.start(
                    grad_in_part, resid_bf, chains["out"].x if k == 0 else out1,
                    v["gelu0"][2 + k], v["gelu1"][2 + k], passage_states, v["states"],
                )
        elif name == "xa":
            v["xa"] = cross(*order.gate(chains["out"].x))
        elif name == "xb":
            v["xb"] = cross(*order.gate(chains["out"].arrived))
        elif name == "ia":
            v["ia"] = cross(*order.gate(chains["inp"].before if chains["inp"].steps == 0 else chains["inp"].x))
        elif name == "ib":
            v["ib"] = cross(*order.gate(chains["inp"].arrived))
        elif name == "wout":
            out1 = weight(chains["out"], "xa", "xb")
        elif name == "win":
            w_in = (chains["inp"].x, weight(chains["inp"], "ia", "ib"))
        elif name in ("nb0", "nb1"):
            k = int(name[2])
            v[name] = swap(order(lambda *w: input_nb((v["p0"], v["p1"]), w, k), *w_in, ticks=0), 1)
        elif name == "own":
            mark = order.mark
            input_grad = order(
                lambda a, b: input_own((v["p0"], v["p1"]), w_in, resid_bf, a, b, mark), v["nb0"], v["nb1"],
                ticks=0,
            )
        elif name in ("tgo", "tgi"):
            pair = [chains[name[1:] + k] for k in "01"]
            pair[0].came, pair[1].came = order.gate(pair[0].came, pair[1].came)
            mark = order.mark
            v[name] = order(lambda *x: total(ids, mark, *pair), pair[0].came, ticks=0)
        else:
            raise ValueError(word)
    return (input_grad, v["tgi"], v["tgo"], question_grad)


def solution(mesh):
    both = P(("groups", "psg"), None)
    return jax.shard_map(
        shards,
        mesh=mesh,
        in_specs=(both, both, both, P("psg", None), P("psg", None), P(), both, both, both, P("groups"), P("groups")),
        out_specs=(both, both, both, both),
        check_vma=False,
    )
```

```python
import functools

import jax
import jax.numpy as jnp
from jax import lax
from jax.experimental import pallas as pl
from jax.experimental.pallas import tpu as pltpu
from jax.sharding import PartitionSpec as P

LEN = 128
TICK = 100_000_000
SCHEDULE = (
    "inp>", "pre>", "resid>", "states>", "out>", "pack", "out:30", "out>", "resid?", "small>",
    "gelu0", "small:1", "small>", "inp:1", "out:1", "out>", "xa", "small:30", "small>", "inp>",
    "gelu1", "small:30", "states?", "small>", "small:1", "ia?", "resid", "out:1", "xb", "xa?",
    "inp:1", "xa?", "inp>", "go1", "ia?", "gi0", "go0", "go0>", "go1>", "gi0>", "inp:1", "wout",
    "gi1:30", "gi1>", "ia", "go0:1", "go0>", "gi0:1", "ia?", "gi0>", "ib", "go1:1", "go1>", "gi1:1",
    "gi1>", "go0:1", "go0>", "gi0:10", "gi0>", "win", "nb0", "go1:1", "go1>", "nb1", "go0?", "tgo",
    "gi1:30", "gi1>", "own", "nb?", "tgi",
)
ORDERS = {"out": "down", "inp": "far", "go0": "side", "go1": "up", "gi0": "far", "gi1": "side"}
BF = jnp.bfloat16
F32 = jnp.float32
PACK_MIB = 63


def params(mib):
    return pltpu.CompilerParams(vmem_limit_bytes=mib << 20)


FREE = pl.CostEstimate(flops=0, bytes_accessed=0, transcendentals=0)


def swap(x, mask):
    n = lax.axis_size("psg")
    return lax.ppermute(x, "psg", [(i, i ^ mask) for i in range(n)])


def pack_kernel(
    slots, ids_ref, place_in, live_in, resid_in, gain_in, query_in, score_in, ret_in, out_ref,
    place_ref, live_ref, resid_ref, gain_ref, query_ref, score_ref, ret_ref, sems,
):
    me = ids_ref[0]
    passages = place_ref.shape[0]
    width = out_ref.shape[1]
    queries, picks = ret_ref.shape
    inputs = (resid_in, place_in, live_in, ret_in, score_in, query_in, gain_in)
    targets = (resid_ref, place_ref, live_ref, ret_ref, score_ref, query_ref, gain_ref)
    small = [pltpu.make_async_copy(a, b, sems.at[i]) for i, (a, b) in enumerate(zip(inputs, targets))]
    for copy in small:
        copy.start()
    for copy in small[1:]:
        copy.wait()
    ids = ret_ref[...]

    def look(i, placed):
        p = place_ref[i]
        owner = p // slots
        slot = p % slots
        rel = (owner ^ me) * slots + slot
        rel = jnp.where(slot < live_ref[owner], rel, -1)
        return jnp.where(ids == i, rel, placed)

    placed = lax.fori_loop(0, passages, look, jnp.full(ids.shape, -1, jnp.int32), unroll=8)
    score = score_ref[...].astype(F32)
    lanes = max(passages, 128)
    cols = lax.broadcasted_iota(jnp.int32, (queries, lanes), 1)
    pairs = jnp.zeros((queries, lanes), F32)
    for k in range(picks):
        pairs = pairs + jnp.where(cols == placed[:, k : k + 1], score[:, k : k + 1], 0.0)
    if lanes < width:
        pairs = jnp.concatenate([pairs, jnp.zeros((queries, width - lanes), F32)], axis=1)
    small[0].wait()
    rows = []
    for s in range(slots):
        x = resid_ref[s * LEN : (s + 1) * LEN, :].astype(F32)
        centre = x - jnp.mean(x, axis=-1, keepdims=True)
        inverse = lax.rsqrt(jnp.mean(centre * centre, axis=-1, keepdims=True) + 1e-06)
        rows.append(jnp.mean(centre * inverse, axis=0, keepdims=True) * gain_ref[...])
    out_ref[...] = jnp.concatenate(rows + [query_ref[...].astype(F32), pairs], axis=0).astype(BF)


def pack(slots, ids, placement, live, resid, gain, query, score, retrieved):
    width = resid.shape[1]
    queries = query.shape[0]
    smem = pl.BlockSpec(memory_space=pltpu.SMEM)
    hbm = pl.BlockSpec(memory_space=pltpu.HBM)
    scratch = [pltpu.SMEM(x.shape, x.dtype) for x in (placement, live)]
    scratch += [pltpu.VMEM(x.shape, x.dtype) for x in (resid, gain, query, score, retrieved)]
    return pl.pallas_call(
        functools.partial(pack_kernel, slots),
        out_shape=jax.ShapeDtypeStruct((slots + 2 * queries, width), BF),
        in_specs=[smem] + [hbm] * 7,
        out_specs=pl.BlockSpec(memory_space=pltpu.VMEM),
        scratch_shapes=scratch + [pltpu.SemaphoreType.DMA((7,))],
        compiler_params=params(PACK_MIB),
        cost_estimate=FREE,
        name="pack",
    )(ids, placement, live, resid, gain, query, score, retrieved)


def resid_kernel(slots, queries, own_ref, nb_ref, all_ref, gain_ref, bf_ref, question_ref, pass_ref):
    step = pl.program_id(0)
    rows = slots + 2 * queries
    total = all_ref.shape[0]
    lanes = max(total // rows * slots, 128)

    @pl.when(step == 0)
    def _():
        table = all_ref[...]
        head = all_ref[:, :lanes].astype(F32)
        r = lax.broadcasted_iota(jnp.int32, (total, lanes), 0)
        c = lax.broadcasted_iota(jnp.int32, (total, lanes), 1)
        inside = r % rows
        moved = pltpu.roll(head, total - queries, 0)
        is_query = (inside >= slots) & (inside < slots + queries)
        fc = lax.broadcasted_iota(jnp.int32, (lanes, 128), 0)
        fs = lax.broadcasted_iota(jnp.int32, (lanes, 128), 1)
        picked = jnp.zeros((total, 128), F32)
        for k in range(2):
            mine = jnp.where(is_query & (c // slots == ((r // rows) ^ k)), moved, 0.0).astype(BF)
            fold = ((fc % slots + k * slots) == fs).astype(F32).astype(BF)
            picked = picked + jnp.dot(mine, fold, preferred_element_type=F32)
        grads = lax.dot_general(
            picked.astype(BF), table, (((0,), (0,)), ((), ())), preferred_element_type=F32
        )
        pass_ref[...] = grads[: 2 * slots] * gain_ref[...] * (1.0 / LEN)
        own = head[:rows]
        ec = lax.broadcasted_iota(jnp.int32, (lanes, total), 0)
        er = lax.broadcasted_iota(jnp.int32, (lanes, total), 1)
        spread = ((er // rows == ec // slots) & (er % rows == ec % slots)).astype(F32).astype(BF)
        weights = jnp.dot(own.astype(BF), spread, preferred_element_type=F32).astype(BF)
        result = jnp.dot(weights, table, preferred_element_type=F32)
        question_ref[...] = result[slots + queries :]

    for part in range(own_ref.shape[0] // LEN):
        here = slice(part * LEN, (part + 1) * LEN)
        for k, src in enumerate((own_ref, nb_ref)):
            x = src[here].astype(F32)
            centre = x - jnp.mean(x, axis=-1, keepdims=True)
            inverse = lax.rsqrt(jnp.mean(centre * centre, axis=-1, keepdims=True) + 1e-06)
            slot = k * slots + step * (own_ref.shape[0] // LEN) + part
            scaled = pass_ref[pl.ds(slot, 1), :]
            base = scaled - jnp.mean(scaled, axis=-1, keepdims=True)
            along = jnp.mean(centre * scaled, axis=-1, keepdims=True) * (inverse * inverse)
            bf_ref[k, here] = (inverse * (base - centre * along)).astype(BF)


def resid_grads(slots, queries, own, nb, table, gain):
    tokens, width = own.shape
    total = table.shape[0]
    block = 4 * LEN
    return pl.pallas_call(
        functools.partial(resid_kernel, slots, queries),
        grid=(tokens // block,),
        out_shape=(
            jax.ShapeDtypeStruct((2, tokens, width), BF),
            jax.ShapeDtypeStruct((queries, width), F32),
        ),
        in_specs=[
            pl.BlockSpec((block, width), lambda s: (s, 0)),
            pl.BlockSpec((block, width), lambda s: (s, 0)),
            pl.BlockSpec((total, width), lambda s: (0, 0)),
            pl.BlockSpec((1, width), lambda s: (0, 0)),
        ],
        out_specs=(
            pl.BlockSpec((2, block, width), lambda s: (0, s, 0)),
            pl.BlockSpec((queries, width), lambda s: (0, 0)),
        ),
        scratch_shapes=[pltpu.VMEM((2 * slots, width), F32)],
        compiler_params=params(16),
        cost_estimate=FREE,
        name="resid_grads",
    )(own, nb, table, gain)


def gelu_kernel(half, ids_ref, in_ref, act0, act1, slope0, slope1):
    chip, core, group = ids_ref[0] // 2, ids_ref[0] % 2, ids_ref[1]
    width = act0.shape[1]
    for i in range(width // 128):
        if half:
            rows = 2 * width // half
            a, b = (
                in_ref[:, pl.ds(pl.multiple_of(((chip ^ j) * 2 + core) * rows, 128), 128)].astype(F32)
                for j in (2 * i, 2 * i + 1)
            )
            low = jnp.concatenate([a[:, :64], b[:, :64]], axis=1)
            high = jnp.concatenate([a[:, 64:], b[:, 64:]], axis=1)
        else:
            low = in_ref[:, i * 128 : (i + 1) * 128].astype(F32)
            high = in_ref[:, width + i * 128 : width + (i + 1) * 128].astype(F32)
        pair = jnp.where(group == 0, low, high), jnp.where(group == 0, high, low)
        for z, act, slope in zip(pair, (act0, act1), (slope0, slope1)):
            cdf = 0.5 * (1.0 + lax.erf(z * 0.7071067811865476))
            density = jnp.exp(-0.5 * z * z) * 0.3989422804014327
            act[:, i * 128 : (i + 1) * 128] = (z * cdf).astype(BF)
            slope[:, i * 128 : (i + 1) * 128] = cdf + z * density


def gelu(ids, preact, units, half):
    tokens, width = preact.shape
    block = 256
    out = pl.BlockSpec((block, units // 2), lambda i, ids: (i, 0))
    return pl.pallas_call(
        functools.partial(gelu_kernel, half),
        grid_spec=pltpu.PrefetchScalarGridSpec(
            num_scalar_prefetch=1,
            grid=(tokens // block,),
            in_specs=[pl.BlockSpec((block, width), lambda i, ids: (i, 0))],
            out_specs=[out] * 4,
        ),
        out_shape=[jax.ShapeDtypeStruct((tokens, units // 2), t) for t in (BF, BF, F32, F32)],
        compiler_params=params(8),
        cost_estimate=FREE,
        name="gelu",
    )(ids, preact)


def grad_out_kernel(rows, own_ref, nb_ref, resid_ref, keep_ref, sent_ref):
    contract = (((0,), (0,)), ((), ()))
    out = lax.dot_general(own_ref[...], resid_ref[0], contract, preferred_element_type=F32)
    out = out + lax.dot_general(nb_ref[...], resid_ref[1], contract, preferred_element_type=F32)
    keep_ref[...], sent_ref[...] = halves(out, rows)


def grad_out_part(rows, own, nb, resid):
    tokens, units = own.shape
    width = resid.shape[2]
    block = 256
    return pl.pallas_call(
        functools.partial(grad_out_kernel, rows),
        grid=(units // block,),
        in_specs=[pl.BlockSpec((tokens, block), lambda j: (0, j))] * 2
        + [pl.BlockSpec((2, tokens, width), lambda j: (0, 0, 0))],
        out_specs=[pl.BlockSpec((block // 2, width), lambda j: (j, 0))] * 2,
        out_shape=[jax.ShapeDtypeStruct((units // 2, width), BF)] * 2,
        compiler_params=params(12),
        cost_estimate=FREE,
        name="grad_out",
    )(own, nb, resid)


def grad_in_kernel(
    rows, resid_ref, w_ref, slope_own, slope_nb, own_ref, nb_ref, pre_ref, keep_ref, sent_ref
):
    total = None
    for k, (slope, states) in enumerate(((slope_own, own_ref), (slope_nb, nb_ref))):
        hidden = lax.dot_general(
            resid_ref[k], w_ref[...], (((1,), (1,)), ((), ())), preferred_element_type=F32
        )
        pre = (hidden * slope[...]).astype(BF)
        pre_ref[k] = pre
        out = lax.dot_general(
            pre, states[...], (((0,), (0,)), ((), ())), preferred_element_type=F32
        )
        total = out if total is None else total + out
    keep_ref[...], sent_ref[...] = halves(total, rows)


def grad_in_part(rows, resid, w_out, slope_own, slope_nb, states, states_nb):
    _, tokens, width = resid.shape
    units = w_out.shape[0]
    block = 256
    whole = lambda j: (0, 0)
    return pl.pallas_call(
        functools.partial(grad_in_kernel, rows),
        grid=(units // block,),
        in_specs=[
            pl.BlockSpec((2, tokens, width), lambda j: (0, 0, 0)),
            pl.BlockSpec((block, width), lambda j: (j, 0)),
            pl.BlockSpec((tokens, block), lambda j: (0, j)),
            pl.BlockSpec((tokens, block), lambda j: (0, j)),
            pl.BlockSpec(states.shape, whole),
            pl.BlockSpec(states.shape, whole),
        ],
        out_specs=(
            pl.BlockSpec((2, tokens, block), lambda j: (0, 0, j)),
            pl.BlockSpec((block // 2, width), lambda j: (j, 0)),
            pl.BlockSpec((block // 2, width), lambda j: (j, 0)),
        ),
        out_shape=(
            jax.ShapeDtypeStruct((2, tokens, units), BF),
            jax.ShapeDtypeStruct((units // 2, width), BF),
            jax.ShapeDtypeStruct((units // 2, width), BF),
        ),
        compiler_params=params(18),
        cost_estimate=FREE,
        name="grad_in",
    )(resid, w_out, slope_own, slope_nb, states, states_nb)


def input_nb_kernel(pre0, pre1, w0, w1, out_ref):
    total = jnp.dot(pre0[0], w0[...], preferred_element_type=F32)
    total = total + jnp.dot(pre1[0], w1[...], preferred_element_type=F32)
    out_ref[...] = total.astype(BF)


def input_own_kernel(pre0, pre1, w0, w1, resid_ref, first_ref, second_ref, mark_ref, out_ref):
    total = jnp.dot(pre0[0], w0[...], preferred_element_type=F32)
    total = total + jnp.dot(pre1[0], w1[...], preferred_element_type=F32)
    total = total + resid_ref[0].astype(F32)

    @pl.when(pl.program_id(0) == 0)
    def _():
        out_ref[...] = (total + first_ref[...].astype(F32)).astype(BF)

    @pl.when(pl.program_id(0) == 1)
    def _():
        out_ref[...] = (total + second_ref[...].astype(F32)).astype(BF)


def input_nb(pre, w_in, part):
    _, tokens, units = pre[0].shape
    width = w_in[0].shape[1]
    block = tokens // 2
    return pl.pallas_call(
        input_nb_kernel,
        grid=(1,),
        in_specs=[pl.BlockSpec((1, block, units), lambda i: (1, part, 0))] * 2
        + [pl.BlockSpec((units, width), lambda i: (0, 0))] * 2,
        out_specs=pl.BlockSpec((block, width), lambda i: (0, 0)),
        out_shape=jax.ShapeDtypeStruct((block, width), BF),
        compiler_params=params(12),
        cost_estimate=FREE,
        name="input_nb",
    )(*pre, *w_in)


def input_own(pre, w_in, resid, first, second, mark):
    _, tokens, units = pre[0].shape
    width = w_in[0].shape[1]
    block = tokens // 2
    whole = lambda i: (0, 0)
    return pl.pallas_call(
        input_own_kernel,
        grid=(2,),
        in_specs=[pl.BlockSpec((1, block, units), lambda i: (0, i, 0))] * 2
        + [pl.BlockSpec((units, width), whole)] * 2
        + [pl.BlockSpec((1, block, width), lambda i: (0, i, 0))]
        + [pl.BlockSpec((block, width), whole)] * 2
        + [pl.BlockSpec(memory_space=pl.ANY)],
        out_specs=pl.BlockSpec((block, width), lambda i: (i, 0)),
        out_shape=jax.ShapeDtypeStruct((tokens, width), BF),
        compiler_params=params(16),
        cost_estimate=FREE,
        name="input_own",
    )(*pre, *w_in, resid, first, second, mark)


def tick_kernel(in_ref, out_ref):
    out_ref[...] = in_ref[...]


def tick(x, count):
    vmem = pl.BlockSpec(memory_space=pltpu.VMEM)
    return pl.pallas_call(
        tick_kernel,
        in_specs=[vmem],
        out_specs=vmem,
        out_shape=jax.ShapeDtypeStruct(x.shape, x.dtype),
        compiler_params=params(1),
        cost_estimate=pl.CostEstimate(flops=count * TICK, bytes_accessed=0, transcendentals=0),
        name="tick",
    )(x)


class Order:
    def __init__(self, mark):
        self.mark = mark

    def gate(self, *args):
        *args, self.mark = lax.optimization_barrier((*args, self.mark))
        return args

    def __call__(self, work, *args, ticks=1):
        out = work(*self.gate(*args))
        leaves, tree = jax.tree.flatten(out)
        out = jax.tree.unflatten(tree, self.gate(*leaves))
        if ticks:
            self.mark = tick(self.mark, ticks)
        return out


def place(mask, masks):
    return sum(1 for other in masks if other > mask)


def run(kernel, name, shapes, *args):
    vmem = pl.BlockSpec(memory_space=pltpu.VMEM)
    return pl.pallas_call(
        kernel,
        in_specs=[vmem] * len(args),
        out_specs=[vmem] * len(shapes),
        out_shape=[jax.ShapeDtypeStruct(s, BF) for s in shapes],
        compiler_params=params(6),
        cost_estimate=FREE,
        name=name,
    )(*args)


def join_kernel(rows, a_ref, b_ref, out_ref):
    total, width = a_ref.shape
    if rows % 16:
        a, b = (x[...].astype(F32).reshape(total // rows, rows, width) for x in (a_ref, b_ref))
        out_ref[...] = jnp.stack([a, b], axis=1).reshape(2 * total, width).astype(BF)
        return
    for i in range(total // rows):
        part = slice(i * rows, (i + 1) * rows)
        out_ref[2 * i * rows : (2 * i + 1) * rows] = a_ref[part]
        out_ref[(2 * i + 1) * rows : (2 * i + 2) * rows] = b_ref[part]


def join(a, b, rows):
    total, width = a.shape
    return run(functools.partial(join_kernel, rows), "join", [(2 * total, width)], a, b)[0]


def halves(x, rows):
    total, width = x.shape
    x = x.reshape(total // (2 * rows), 2, rows, width)
    return [x[:, k].reshape(total // 2, width).astype(BF) for k in range(2)]


def fold_kernel(rows, a_ref, b_ref, keep_ref, sent_ref):
    total = a_ref[...].astype(F32) + b_ref[...].astype(F32)
    keep_ref[...], sent_ref[...] = halves(total, rows)


def fold(a, b, rows):
    total, width = a.shape
    return run(functools.partial(fold_kernel, rows), "fold", [(total // 2, width)] * 2, a, b)


def total_kernel(ids_ref, *refs):
    *parts, mark_ref, out_ref, sum_ref, sems = refs
    rows = sum_ref.shape[1]
    copies = []
    for k in range(2):
        sum_ref[k] = parts[2 * k][...].astype(F32) + parts[2 * k + 1][...].astype(F32)
        start = k * rows + (1 - 2 * k) * ids_ref[1] * rows
        there = out_ref.at[pl.ds(pl.multiple_of(start, rows), rows)]
        copies.append(pltpu.make_async_copy(sum_ref.at[k], there, sems.at[k]))
        copies[k].start()
    for copy in copies:
        copy.wait()


def total(ids, mark, *chains):
    parts = [x for chain in chains for x in (chain.keep, chain.came)]
    rows = sum(chain.keep.shape[0] for chain in chains)
    vmem = pl.BlockSpec(memory_space=pltpu.VMEM)
    return pl.pallas_call(
        total_kernel,
        in_specs=[pl.BlockSpec(memory_space=pltpu.SMEM)] + [vmem] * (len(parts) + 1),
        out_specs=pl.BlockSpec(memory_space=pl.ANY),
        scratch_shapes=[pltpu.VMEM((2, rows // 2, parts[0].shape[1]), F32), pltpu.SemaphoreType.DMA((2,))],
        out_shape=jax.ShapeDtypeStruct((rows, parts[0].shape[1]), F32),
        compiler_params=params(6),
        cost_estimate=FREE,
        name="total",
    )(ids, *parts, mark)


class Chain:
    def __init__(self, order, masks, rows):
        self.order, self.left, self.done, self.rows = order, list(masks), [], rows
        self.steps = 3

    def due(self, last):
        self.steps -= 1
        while len(self.left) > max(self.steps, last):
            yield self.left[0]


class Gather(Chain):
    def __init__(self, order, x, masks):
        super().__init__(order, masks, x.shape[0])
        self.x = x
        self.steps = min(len(self.left), 4 if masks[-1] == 1 else 3)

    def send(self):
        self.came = swap(*self.order.gate(self.x), self.left[0])

    def step(self, ticks):
        first = True
        for mask in self.due(0):
            if not first:
                self.send()
            first = False
            rows = self.rows << (len(self.done) - place(mask, self.done))
            self.before, self.arrived, self.block = self.x, self.came, rows
            self.x = self.order(lambda a, b: join(a, b, rows), self.x, self.came, ticks=ticks)
            self.done.append(self.left.pop(0))


class Scatter(Chain):
    def block(self):
        return self.rows << (len(self.left) - 1 - place(self.left[0], self.left))

    def start(self, make, *args):
        rows = self.block()
        *extra, self.keep, self.sent = self.order(lambda *x: make(rows, *x), *args, ticks=0)
        return extra

    def send(self):
        self.came = swap(*self.order.gate(self.sent), self.left[0])

    def step(self, ticks):
        first = True
        for _ in self.due(1):
            if not first:
                self.send()
            first = False
            self.left.pop(0)
            rows = self.block()
            self.keep, self.sent = self.order(
                lambda a, b: fold(a, b, rows), self.keep, self.came, ticks=ticks
            )


def shards(
    passage_states,
    saved_preact,
    saved_resid,
    w_in,
    w_out,
    norm_gain,
    query_emb,
    score_grads,
    retrieved,
    placement_map,
    live_counts,
):
    n = lax.axis_size("psg")
    shared = lax.axis_size("groups") == 2
    me = lax.axis_index("psg").astype(jnp.int32)
    group = lax.axis_index("groups").astype(jnp.int32) if shared else jnp.int32(0)
    ids = jnp.stack([me, group])
    core, chip = me % 2, me // 2
    half = n // 2
    tokens, width = saved_resid.shape
    rows = w_in.shape[0]
    units = half * rows
    slots = tokens // LEN
    queries = query_emb.shape[0]
    masks = [1 << b for b in range(1, n.bit_length() - 1)]
    orders = {
        "up": masks,
        "down": masks[::-1],
        "side": masks[1::-1] + masks[2:],
        "far": masks[:1] + masks[:0:-1],
        "mixed": masks[1:2] + masks[:1:-1] + masks[:1],
        "low": masks[:1:-1] + masks[:2],
    }
    gain = norm_gain.reshape(1, width)
    whole_tiles = rows == 128
    order = Order(jnp.zeros((8, 128), F32) + me.astype(F32))

    def cross(x):
        return lax.ppermute(x, "groups", [(0, 1), (1, 0)])

    preact_own = columns = saved_preact
    if not whole_tiles:
        view = saved_preact.reshape(tokens, half, 2, 2, rows // 2)
        view = jnp.take(view, jnp.arange(half) ^ chip, axis=1).transpose(2, 0, 3, 1, 4)
        view = view.reshape(2, tokens, units)
        preact_own = lax.dynamic_index_in_dim(view, core, axis=0, keepdims=False)
        columns = lax.dynamic_index_in_dim(view, 1 - core, axis=0, keepdims=False)
    mine_out, mine_in = (
        lax.dynamic_slice_in_dim(w, group * (rows // 2), rows // 2, 0) for w in (w_out, w_in)
    )
    v, swapped = {}, {"pre": columns, "resid": saved_resid, "states": passage_states}
    chains = {
        "out": Gather(order, mine_out, orders[ORDERS["out"]]),
        "inp": Gather(order, mine_in, orders[ORDERS["inp"]]),
    }
    for name in ("go0", "go1", "gi0", "gi1"):
        chains[name] = Scatter(order, orders[ORDERS[name]], rows // 2)

    def weight(chain, first, second):
        return order(lambda a, b: join(a, b, chain.block), v.pop(first), v.pop(second), ticks=0)

    for word in SCHEDULE:
        name, _, ticks = word.partition(":")
        ticks = int(ticks or 0)
        chain = chains.get(name.rstrip(">"))
        if name[:-1] in swapped and name.endswith(">"):
            x = swapped[name[:-1]]
            v[name[:-1]] = swap(*order.gate(x), 1) if ticks else swap(x, 1)
        elif name.endswith(">"):
            chain.send()
        elif name.endswith("?"):
            if name[:-1] in chains:
                chain = chains[name[:-1]]
                chain.came, = order.gate(chain.came)
            for key in [k for k in v if k.startswith(name[:-1])]:
                v[key], = order.gate(v[key])
            if ticks:
                order.mark = tick(order.mark, ticks)
        elif name in ("out", "inp", "small"):
            chain.step(ticks)
        elif name == "pack":
            table = order(
                lambda *args: pack(slots, ids, *args),
                placement_map, live_counts, saved_resid, gain, query_emb, score_grads, retrieved, ticks=0,
            )
            chains["small"] = Gather(order, table, orders["far"] + [1])
        elif name in ("gelu0", "gelu1"):
            x = preact_own if name == "gelu0" else v["pre"]
            v[name] = order(lambda x: gelu(ids, x, units, half if whole_tiles else 0), x, ticks=0)
        elif name == "resid":
            resid_bf, question_grad = order(
                lambda a, b, c: resid_grads(slots, queries, a, b, c, gain),
                saved_resid, v["resid"], chains["small"].x, ticks=0,
            )
        elif name in ("go0", "go1", "gi0", "gi1"):
            k = int(name[2])
            if chain.steps < 3 or hasattr(chain, "keep"):
                chain.step(ticks)
            elif name[:2] == "go":
                chain.start(grad_out_part, v["gelu0"][k], v["gelu1"][k], resid_bf)
            else:
                v["p%d" % k], = chain.start(
                    grad_in_part, resid_bf, chains["out"].x if k == 0 else out1,
                    v["gelu0"][2 + k], v["gelu1"][2 + k], passage_states, v["states"],
                )
        elif name == "xa":
            v["xa"] = cross(*order.gate(chains["out"].x))
        elif name == "xb":
            v["xb"] = cross(*order.gate(chains["out"].arrived))
        elif name == "ia":
            v["ia"] = cross(*order.gate(chains["inp"].before if chains["inp"].steps == 0 else chains["inp"].x))
        elif name == "ib":
            v["ib"] = cross(*order.gate(chains["inp"].arrived))
        elif name == "wout":
            out1 = weight(chains["out"], "xa", "xb")
        elif name == "win":
            w_in = (chains["inp"].x, weight(chains["inp"], "ia", "ib"))
        elif name in ("nb0", "nb1"):
            k = int(name[2])
            v[name] = swap(order(lambda *w: input_nb((v["p0"], v["p1"]), w, k), *w_in, ticks=0), 1)
        elif name == "own":
            mark = order.mark
            input_grad = order(
                lambda a, b: input_own((v["p0"], v["p1"]), w_in, resid_bf, a, b, mark), v["nb0"], v["nb1"],
                ticks=0,
            )
        elif name in ("tgo", "tgi"):
            pair = [chains[name[1:] + k] for k in "01"]
            pair[0].came, pair[1].came = order.gate(pair[0].came, pair[1].came)
            mark = order.mark
            v[name] = order(lambda *x: total(ids, mark, *pair), pair[0].came, ticks=0)
        else:
            raise ValueError(word)
    return (input_grad, v["tgi"], v["tgo"], question_grad)


def solution(mesh):
    both = P(("groups", "psg"), None)
    return jax.shard_map(
        shards,
        mesh=mesh,
        in_specs=(both, both, both, P("psg", None), P("psg", None), P(), both, both, both, P("groups"), P("groups")),
        out_specs=(both, both, both, both),
        check_vma=False,
    )
```
